256 devices in a mesh: dp: 64 (over z_lo, y, x, core), tensor: 4 (over z_hi).
Axes of the slice: x: 4, y: 4, z: 8 (z_hi: 4, z_lo: 2; z = z_hi * 2 + z_lo), core: 2. Of those that a mesh axis runs over, the one named last changes fastest.
Arguments:
- queries: bfloat16 [4, 2, 256, 8192], P(None, None, 'dp', 'tensor'), may hold values from -125 to 125
- fresh_kv: bfloat16 [4, 2, 256, 2, 1024], P(None, None, 'dp', None, 'tensor'), may hold values from -4.5 to 4.5
- kv_cache: bfloat16 [2, 256, 512, 2, 1024], P(None, 'dp', None, None, 'tensor'), may hold values from -6 to 6
- cache_len: int32 [256], P('dp'), may hold values from 1 to 512, 81920 in all
- out_proj: bfloat16 [2, 8192, 8192], P(None, 'tensor', 'dp'), may hold values from -0.5 to 0.5
- finished: int32 [256], P('dp'), may hold values 0 or 1
- resp_len: int32 [256], P('dp'), may hold values from 1 to 128, 20480 in all
- start_shard: int32 [256], P('dp'), may hold values from 0 to 3
- resp_act: bfloat16 [256, 128, 8192], P('dp', None, 'tensor'), may hold values from -130 to 130
- reward_gain: bfloat16 [8192], P('tensor'), may hold values from 0.099609375 to 1.8984375
- reward_weight: bfloat16 [8192, 2048], P('tensor', 'dp'), may hold values from -0.0625 to 0.0625
Outputs:
- decoded: bfloat16 [4, 256, 8192], P(None, 'dp')
- scored: bfloat16 [32768, 2048], P('dp', 'tensor')
The draws below stay inside these ranges and needn't reach their ends.
All inputs are finite; a program needn't handle non-finite values. No bound on the sum of `cache_len` or of `finished` or of `resp_len` on one device may be relied on, other than what follows from the above.
Results may differ from the reference program's by a relative error of at most 0.0057.
Values may be sent and summed in bfloat16 or wider, within the bound.
A program may use at most 128 MiB of HBM per device.

```python
import math
import jax
import jax.numpy as jnp
import numpy as np
from jax import lax

D = 8192
HEADS = 64
KV_HEADS = 8
HEAD = 128
CACHE = 512
ROWS_G = 4
RESP = 128
STEPS = 4
LAYERS = 2
SPREAD = 4
QW = 8192
KVW = 1024
OUTW = 2048
ROWS = 256
QUART = 32
N_DP = 64


def shared_align(key):
    first = jax.random.fold_in(key, 0)
    base = jnp.clip(jax.random.normal(first, (STEPS, LAYERS, ROWS, 2, KV_HEADS * HEAD), jnp.float32), -4.5, 4.5)
    return base


def draw_fresh_kv(key, part):
    base = shared_align(key)
    return base.astype(jnp.bfloat16)


def draw_queries(key, part):
    key = jax.random.fold_in(key, 12)
    drawn = jnp.clip(jax.random.normal(key, (STEPS, LAYERS, ROWS, HEADS * HEAD), jnp.float32), -6.0, 6.0)
    return drawn.astype(jnp.bfloat16)


def draw_resp_act(key, part):
    key = jax.random.fold_in(key, 14)
    first, second, third = jax.random.split(key, 3)
    columns = jnp.arange(D, dtype=jnp.float32) / D
    wobble = jnp.exp(jax.random.uniform(second, (D,), jnp.float32, -0.35, 0.35))
    row_scale = jnp.exp(jax.random.uniform(third, (ROWS, RESP, 1), jnp.float32, 0.0, math.log(10.0)))
    values = jnp.clip(jax.random.normal(first, (ROWS, RESP, D), jnp.float32), -5.0, 5.0)
    col_scale = 0.6 * jnp.power(3.0, columns) * wobble
    return (values * col_scale[None, None, :] * row_scale).astype(jnp.bfloat16)


def set_ends(values, stream_key, least, top_value):
    dims = values.shape
    spot = [jax.random.randint(jax.random.fold_in(stream_key, axis), (), 0, dims[axis]) for axis in range(len(dims))]
    values = values.at[tuple(spot)].set(least)
    longest = dims.index(max(dims))
    spot[longest] = (spot[longest] + 1) % dims[longest]
    return values.at[tuple(spot)].set(top_value)


def level_of(rng, shape, pieces, least, largest):
    def one(dim, blocks):
        heights = jax.random.uniform(jax.random.fold_in(jax.random.fold_in(rng, 6), dim), (blocks,), jnp.float32, least / len(pieces), largest / len(pieces))
        return jnp.repeat(jnp.exp(heights), shape[dim] // blocks).reshape((-1,) + (1,) * (len(shape) - dim - 1))

    factor_of = one(*pieces[0])
    for cut in pieces[1:]:
        factor_of = factor_of * one(*cut)
    return factor_of


def length_profile(number_of, total, limit, slope):
    portions = [(1 << 20) // math.isqrt(grade ** slope) + 1 for grade in range(2, number_of + 1)]
    spare, counts = total - limit - (number_of - 1), [1] * (number_of - 1)
    while spare > 0:
        candidates = [i for i in range(number_of - 1) if counts[i] < limit]
        pool, left = sum([portions[i] for i in candidates]), spare
        for i in candidates:
            extra = min(limit - counts[i], max(1, left * portions[i] // pool), spare)
            counts[i] = counts[i] + extra
            spare = spare - extra
    return np.array([limit] + counts)


def uneven(stream_key, count, total, reach, skew):
    if count == 2:
        one = jax.random.randint(stream_key, (), max(1, total - reach), min(reach, total - 1) + 1)
        return jnp.stack([one, total - one])
    lengths = jnp.asarray(length_profile(count, total, reach, skew), jnp.int32)
    twos = (count - 1) // 2
    giver, taker = lengths[1:1 + 2 * twos:2], lengths[2:2 + 2 * twos:2]
    margin = jnp.minimum(giver - 1, reach - taker)
    shifted = jax.random.randint(jax.random.fold_in(stream_key, 1), (twos,), 0, 1 << 20) % (margin + 1)
    lengths = lengths.at[1:1 + 2 * twos:2].set(giver - shifted).at[2:2 + 2 * twos:2].set(taker + shifted)
    return lengths[jax.random.permutation(jax.random.fold_in(stream_key, 2), count)]


def normal_values(key, dims, spread, most, cuts=(), held_as=jnp.bfloat16):
    values = spread * jax.random.normal(key, dims, jnp.float32)
    if cuts:
        values = values * level_of(key, dims, cuts, -0.22, 0.18)
    return jnp.clip(values, -most, most).astype(held_as)


def setup_inputs(seed: int = 0) -> dict:
    seeds = jax.random.split(jax.random.key(seed), 12)
    queries = draw_queries(jax.random.fold_in(seeds[11], 71), 0)
    fresh_kv = draw_fresh_kv(jax.random.fold_in(seeds[11], 71), 0)
    kv_cache = normal_values(seeds[2], (LAYERS, ROWS, CACHE, 2, KVW), 1.0, 6.0, ((1, 64), (4, 4)))
    cache_len = uneven(seeds[3], ROWS, ROWS * CACHE * 5 // 8, CACHE, 1).astype(jnp.int32)
    out_proj = normal_values(seeds[4], (LAYERS, QW, D), (QW // 64) ** -0.5, 0.5, ((1, 4), (2, 64)))
    finished = set_ends((jax.random.randint(seeds[5], (ROWS,), 0, 4) < 3).astype(jnp.int32), jax.random.fold_in(seeds[5], 1), 0, 1)
    resp_len = uneven(seeds[6], ROWS, ROWS * RESP * 5 // 8, RESP, 1).astype(jnp.int32)
    start_shard = set_ends(jax.random.randint(seeds[7], (ROWS,), 0, SPREAD), jax.random.fold_in(seeds[7], 1), 0, SPREAD - 1).astype(jnp.int32)
    resp_act = draw_resp_act(jax.random.fold_in(seeds[11], 71), 0)
    reward_gain = jnp.clip(1.0 + 0.18 * jax.random.normal(seeds[9], (D,), jnp.float32), 0.099609375, 1.8984375).astype(jnp.bfloat16)
    reward_weight = normal_values(seeds[10], (D, OUTW), D ** -0.5, 0.0625, ((0, 4), (1, 64)))
    return dict(queries=queries, fresh_kv=fresh_kv, kv_cache=kv_cache, cache_len=cache_len, out_proj=out_proj, finished=finished, resp_len=resp_len, start_shard=start_shard, resp_act=resp_act, reward_gain=reward_gain, reward_weight=reward_weight)


epsilon = 1e-05
masked_score = -1e+30

def attend(query, cache_keys, cache_vals, valid_cache, fresh_keys, fresh_vals, valid_fresh):
    scale = 1.0 / math.sqrt(query.shape[-1])
    query_f = query.astype(jnp.float32)
    cache_scores = jnp.einsum('rkgd,rpkd->rkgp', query_f, cache_keys.astype(jnp.float32)) * scale
    fresh_scores = jnp.einsum('rkgd,rpkd->rkgp', query_f, fresh_keys.astype(jnp.float32)) * scale
    cache_scores = jnp.where(valid_cache[:, None, None, :], cache_scores, masked_score)
    fresh_scores = jnp.where(valid_fresh[:, None, None, :], fresh_scores, masked_score)
    peak = jnp.maximum(cache_scores.max(-1), fresh_scores.max(-1))[..., None]
    cache_exp = jnp.exp(cache_scores - peak)
    fresh_exp = jnp.exp(fresh_scores - peak)
    total = cache_exp.sum(-1, keepdims=True) + fresh_exp.sum(-1, keepdims=True)
    cache_w = (cache_exp / total).astype(jnp.bfloat16)
    fresh_w = (fresh_exp / total).astype(jnp.bfloat16)
    result = jnp.einsum('rkgp,rpkd->rkgd', cache_w.astype(jnp.float32), cache_vals.astype(jnp.float32))
    result = result + jnp.einsum('rkgp,rpkd->rkgd', fresh_w.astype(jnp.float32), fresh_vals.astype(jnp.float32))
    return result.astype(jnp.bfloat16).reshape(query.shape[0], -1)

def reference(queries, fresh_kv, kv_cache, cache_len, out_proj, finished, resp_len, start_shard, resp_act, reward_gain, reward_weight):
    group = HEADS // KV_HEADS
    rows_all = queries.shape[2]
    valid_cache = jnp.arange(CACHE, dtype=jnp.int32)[None, :] < cache_len[:, None]
    outputs = []
    for step_no in range(STEPS):
        valid_fresh = jnp.broadcast_to(jnp.arange(STEPS, dtype=jnp.int32) <= step_no, (rows_all, STEPS))
        total = jnp.zeros((rows_all, D), jnp.float32)
        for layer_no in range(LAYERS):
            query = queries[step_no, layer_no].reshape(rows_all, KV_HEADS, group, HEAD)
            cache_keys = kv_cache[layer_no, :, :, 0].reshape(rows_all, CACHE, KV_HEADS, HEAD)
            cache_vals = kv_cache[layer_no, :, :, 1].reshape(rows_all, CACHE, KV_HEADS, HEAD)
            fresh = jnp.swapaxes(fresh_kv[:, layer_no], 0, 1)
            fresh_keys = fresh[:, :, 0].reshape(rows_all, STEPS, KV_HEADS, HEAD)
            fresh_vals = fresh[:, :, 1].reshape(rows_all, STEPS, KV_HEADS, HEAD)
            heads_out = attend(query, cache_keys, cache_vals, valid_cache, fresh_keys, fresh_vals, valid_fresh)
            total = total + jnp.dot(heads_out, out_proj[layer_no], preferred_element_type=jnp.float32)
        outputs.append(total.astype(jnp.bfloat16))
    decoded = jnp.stack(outputs)
    live = (finished[:, None] == 1) & (jnp.arange(RESP, dtype=jnp.int32)[None, :] < resp_len[:, None])
    masked = resp_act * live[:, :, None].astype(resp_act.dtype)

    def score_row(row):
        floats = row.astype(jnp.float32)
        scale = lax.rsqrt(lax.optimization_barrier(jnp.mean(floats * floats, axis=-1)) + epsilon)
        normed = (floats * scale[:, None] * reward_gain.astype(jnp.float32)).astype(jnp.bfloat16)
        return jnp.dot(normed, reward_weight, preferred_element_type=jnp.float32).astype(jnp.bfloat16)
    projected = lax.map(score_row, masked)
    dest = jnp.arange(N_DP, dtype=jnp.int32)[:, None, None, None]
    offset = jnp.arange(SPREAD, dtype=jnp.int32)[None, :, None, None]
    local_row = jnp.arange(ROWS_G, dtype=jnp.int32)[None, None, :, None]
    within = jnp.arange(QUART, dtype=jnp.int32)[None, None, None, :]
    source = jnp.mod(dest - offset, N_DP) * ROWS_G + local_row
    block = jnp.mod(offset - start_shard[source], SPREAD)
    column = block * QUART + within
    source_full = jnp.broadcast_to(source, column.shape)
    scored = projected[source_full, column].reshape(ROWS * RESP, OUTW)
    return (decoded, scored)
```

```python
import math

import jax
import jax.numpy as jnp
from jax import lax
from jax.sharding import PartitionSpec as P

HEAD = 128
SPREAD = 4


epsilon = 1e-05
masked_score = -1e30


def shifted(block, axis, distance):
    devices = range(lax.axis_size(axis))
    route = [((i - distance) % len(devices), i) for i in devices]
    return lax.ppermute(block, axis, route)


def attend(queries, fresh_kv, kv_cache, cache_len):
    steps, layers, rows, width = queries.shape
    cache = kv_cache.shape[2]
    kvs = kv_cache.shape[-1] // HEAD
    group = width // (kvs * HEAD)
    scale = 1.0 / math.sqrt(HEAD)
    q = queries.reshape(steps, layers, rows, kvs, group, HEAD)
    c = kv_cache.reshape(layers, rows, cache, 2, kvs, HEAD)
    f = fresh_kv.reshape(steps, layers, rows, 2, kvs, HEAD)
    cs = jnp.einsum("slrkgd,lrpkd->lrksgp", q, c[:, :, :, 0], preferred_element_type=jnp.float32) * scale
    fs = jnp.einsum("slrkgd,ulrkd->lrksgu", q, f[:, :, :, 0], preferred_element_type=jnp.float32) * scale
    valid = jnp.arange(cache, dtype=jnp.int32)[None, :] < cache_len[:, None]
    cs = jnp.where(valid[None, :, None, None, None, :], cs, masked_score)
    order = jnp.arange(steps, dtype=jnp.int32)
    seen = order[None, :] <= order[:, None]
    fs = jnp.where(seen[None, None, None, :, None, :], fs, masked_score)
    peak = jnp.maximum(cs.max(-1), fs.max(-1))[..., None]
    ce = jnp.exp(cs - peak)
    fe = jnp.exp(fs - peak)
    total = ce.sum(-1, keepdims=True) + fe.sum(-1, keepdims=True)
    cw = (ce / total).astype(jnp.bfloat16)
    fw = (fe / total).astype(jnp.bfloat16)
    out = jnp.einsum("lrksgp,lrpkd->rslkgd", cw, c[:, :, :, 1], preferred_element_type=jnp.float32)
    out = out + jnp.einsum("lrksgu,ulrkd->rslkgd", fw, f[:, :, :, 1], preferred_element_type=jnp.float32)
    return out.astype(jnp.bfloat16).reshape(rows * steps, layers * width)


def shards(
    queries,
    fresh_kv,
    kv_cache,
    cache_len,
    out_proj,
    finished,
    resp_len,
    start_shard,
    resp_act,
    reward_gain,
    reward_weight,
):
    steps, layers, rows, width = queries.shape
    groups = lax.axis_size("dp")
    heads = attend(queries, fresh_kv, kv_cache, cache_len)
    weight = lax.all_gather(reward_weight, "dp", axis=1, tiled=True)
    heads = lax.all_gather(heads, "dp", axis=0, tiled=True)
    part = jnp.dot(heads, out_proj.reshape(layers * width, -1), preferred_element_type=jnp.float32)
    summed = lax.psum(part, "tensor").astype(jnp.bfloat16)
    moved = lax.all_to_all(
        summed.reshape(groups, rows, steps, -1), "dp", split_axis=0, concat_axis=0, tiled=True
    )
    decoded = moved.transpose(2, 1, 0, 3).reshape(steps, rows, -1)

    count = resp_act.shape[1]
    quart = count // SPREAD
    live = (finished[:, None] == 1) & (
        jnp.arange(count, dtype=jnp.int32)[None, :] < resp_len[:, None]
    )
    masked = resp_act * live[:, :, None].astype(resp_act.dtype)
    folded = masked.reshape(rows, SPREAD, quart, -1)
    offset = jnp.arange(SPREAD, dtype=jnp.int32)
    block = jnp.mod(offset[None, :] - start_shard[:, None], SPREAD)
    turned = jnp.take_along_axis(folded, block[:, :, None, None], axis=1)
    turned = turned.transpose(1, 0, 2, 3).reshape(SPREAD * rows * quart, -1)
    floats = turned.astype(jnp.float32)
    squares = lax.psum(jnp.sum(floats * floats, axis=-1), "tensor")
    features = turned.shape[-1] * lax.axis_size("tensor")
    scale = lax.rsqrt(squares / features + epsilon)
    normed = (floats * scale[:, None] * reward_gain.astype(jnp.float32)).astype(jnp.bfloat16)
    cols = jnp.dot(normed, weight, preferred_element_type=jnp.float32)
    mine = lax.psum_scatter(cols, "tensor", scatter_dimension=1, tiled=True).astype(jnp.bfloat16)
    mine = mine.reshape(SPREAD, rows * quart, -1)
    scored = jnp.concatenate([mine[0]] + [shifted(mine[k], "dp", k) for k in range(1, SPREAD)])
    return (decoded, scored)


def solution(mesh):
    return jax.shard_map(
        shards,
        mesh=mesh,
        in_specs=(
            P(None, None, "dp", "tensor"),
            P(None, None, "dp", None, "tensor"),
            P(None, "dp", None, None, "tensor"),
            P("dp"),
            P(None, "tensor", "dp"),
            P("dp"),
            P("dp"),
            P("dp"),
            P("dp", None, "tensor"),
            P("tensor"),
            P("tensor", "dp"),
        ),
        out_specs=(P(None, "dp", None), P("dp", "tensor")),
        check_vma=False,
    )
```

```python
import functools
import math

import jax
import jax.numpy as jnp
from jax import lax
from jax.experimental import pallas as pl
from jax.experimental.pallas import tpu as pltpu
from jax.sharding import PartitionSpec as P

HEAD = 128
SPREAD = 4
QUART = 32
ROWS_G = 4
TENSOR = 4

epsilon = 1e-05
masked_score = -1e30

MESH = pl.DeviceIdType.MESH
STEP_OFF = (0, 1, -1, 2)
BACK = {1: 2, -1: 1, 2: 3}
F32 = jnp.float32
BF16 = jnp.bfloat16


def wrap(v, n):
    return lax.rem(v + 2 * n, n)


class Place:
    def __init__(self):
        self.dp = lax.axis_index("dp")
        self.t = lax.axis_index("tensor")
        self.core = lax.rem(self.dp, 2)
        self.x = lax.rem(self.dp // 2, 4)
        self.y = lax.rem(self.dp // 8, 4)
        self.zl = self.dp // 32

    def at(self, zl, y, x, core):
        return (((zl * 4 + y) * 4 + x) * 2 + core, self.t)


class Gather:
    def __init__(self, place, own, out, send, recv, local):
        self.p, self.own, self.out, self.send, self.recv, self.local = place, own, out, send, recv, local

    def ring(self, h):
        return (self.p.y, self.p.x) if h == 0 else (self.p.x, self.p.y)

    def dev(self, h, s, f, zl=None, core=None):
        p = self.p
        zl = p.zl if zl is None else zl
        core = p.core if core is None else core
        return p.at(zl, s, f, core) if h == 0 else p.at(zl, f, s, core)

    def unit(self, h, j, core=None):
        s, f = self.ring(h)
        s = wrap(s + STEP_OFF[j // 4], 4)
        f = wrap(f + STEP_OFF[j % 4], 4)
        return self.out.at[h, s, f, :, self.p.core if core is None else core]

    def copy(self, h, src, dst, send, recv, dev):
        return pltpu.make_async_remote_copy(
            src_ref=src, dst_ref=dst, send_sem=self.send.at[h, send], recv_sem=self.recv.at[h, recv],
            device_id=dev, device_id_type=MESH)

    def z_copy(self, h):
        s, f = self.ring(h)
        return self.copy(h, self.own(h), self.out.at[h, s, f, self.p.zl, self.p.core], 0, 0,
                         self.dev(h, s, f, zl=1 - self.p.zl))

    def own_copy(self, h):
        s, f = self.ring(h)
        return pltpu.make_async_copy(self.own(h), self.out.at[h, s, f, self.p.zl, self.p.core], self.local.at[h])

    def start(self):
        for h in range(2):
            self.z_copy(h).start()
            self.own_copy(h).start()

    def first(self, h, i):
        s, f = self.ring(h)
        u = self.unit(h, 0)
        return self.copy(h, u, u, i, BACK[STEP_OFF[i]], self.dev(h, s, wrap(f + STEP_OFF[i], 4)))

    def second(self, h, i, right):
        s, f = self.ring(h)
        u = self.unit(h, i)
        step = 1 if right else -1
        base = 8 if right else 4
        return self.copy(h, u, u, base + i, base + i, self.dev(h, wrap(s + step, 4), f))

    def onward(self, h, i):
        s, f = self.ring(h)
        u = self.unit(h, (8 if i < 2 else 4) + i)
        return self.copy(h, u, u, 12 + i, 12 + i, self.dev(h, wrap(s + (1 if i < 2 else -1), 4), f))

    def across(self, h, j):
        s, f = self.ring(h)
        u = self.unit(h, j)
        return self.copy(h, u, u, 16 + j, 16 + j, self.dev(h, s, f, core=1 - self.p.core))

    def arrived(self, h, j):
        u = self.unit(h, j)
        self.copy(h, u, u, j, j, self.dev(h, *self.ring(h), core=1 - self.p.core)).wait_recv()

    def after_z(self):
        for h in range(2):
            s, f = self.ring(h)
            u = self.out.at[h, s, f, 1 - self.p.zl, self.p.core]
            self.copy(h, u, u, 0, 0, self.dev(h, s, f, zl=1 - self.p.zl)).wait_recv()
            self.own_copy(h).wait()
            for i in (1, 2, 3):
                self.first(h, i).start()
            for right in (True, False):
                self.second(h, 0, right).start()
            self.across(h, 0).start()

    def after_first(self, i):
        for h in range(2):
            self.arrived(h, i)
            for right in (True, False):
                self.second(h, i, right).start()
            self.across(h, i).start()

    def after_second(self, i):
        for h in range(2):
            for j in ((8 + i, 4 + i) if i < 2 else (4 + i, 8 + i)):
                self.arrived(h, j)
                if j == (8 if i < 2 else 4) + i:
                    self.onward(h, i).start()
                self.across(h, j).start()

    def after_onward(self, i):
        for h in range(2):
            self.arrived(h, 12 + i)
            self.across(h, 12 + i).start()

    def after_across(self):
        for h in range(2):
            for j in range(16):
                u = self.unit(h, j, core=1 - self.p.core)
                self.copy(h, u, u, 16 + j, 16 + j, self.dev(h, *self.ring(h), core=1 - self.p.core)).wait_recv()

    def end(self):
        for h in range(2):
            self.z_copy(h).wait_send()
            for i in (1, 2, 3):
                self.first(h, i).wait_send()
            for i in range(4):
                self.second(h, i, True).wait_send()
                self.second(h, i, False).wait_send()
                self.onward(h, i).wait_send()
            for j in range(16):
                self.across(h, j).wait_send()


def eye_mask():
    return lax.broadcasted_iota(jnp.int32, (128, 128), 0) == lax.broadcasted_iota(jnp.int32, (128, 128), 1)


def dot_nt(a, b):
    return lax.dot_general(a, b, (((1,), (1,)), ((), ())), preferred_element_type=F32)


def kernel(
    pick_ref, heads_ref, outp_ref, resp_ref, gain_ref, wt_ref,
    dec_ref, scored_ref,
    gw, gh, normed, pacc, rs_send, rs_recv, dacc, ds_send, ds_recv, dfin, sq_own, sq_got,
    w_send, w_recv, w_local, h_send, h_recv, h_local,
    rss, rsr, dss, dsr, sqs, sqr, rot_s, rot_r, out_s, out_r,
):
    p = Place()
    dp, t = p.dp, p.t
    groups = 64
    width = wt_ref.shape[1]
    half_w = width // 2
    is_self = lax.div(dp, 16) == t

    barrier = pltpu.get_barrier_semaphore()

    def greet(dev):
        pl.semaphore_signal(barrier, inc=1, device_id=dev, device_id_type=MESH)

    greet(p.at(1 - p.zl, p.y, p.x, p.core))
    greet(p.at(p.zl, p.y, p.x, 1 - p.core))
    for d in (1, 2, 3):
        greet(p.at(p.zl, p.y, wrap(p.x + d, 4), p.core))
        greet(p.at(p.zl, wrap(p.y + d, 4), p.x, p.core))
        greet((dp, wrap(t + d, 4)))
        greet((wrap(dp - d, groups), t))

    def greet_source(d, c):
        src_t = lax.div(dp, 16)

        @pl.when(jnp.logical_not(jnp.logical_and(d == dp, src_t == t)))
        def _():
            greet((d, src_t))

        return c

    lax.fori_loop(0, groups, greet_source, 0)
    pl.semaphore_wait(barrier, 14 + groups - is_self.astype(jnp.int32))

    gath_w = Gather(p, lambda h: wt_ref.at[:, pl.ds(h * half_w, half_w)], gw, w_send, w_recv, w_local)
    gath_h = Gather(p, lambda h: heads_ref.at[:, pl.ds(h * width, width)], gh, h_send, h_recv, h_local)
    gath_w.start()
    gath_h.start()

    eye = eye_mask()

    def turn_rows(r, c):
        col = jnp.zeros((128, 1), F32)
        for part in range(4):
            cols = slice(part * (width // 4), (part + 1) * (width // 4))
            block = jnp.dot(pick_ref[r], resp_ref[r, :, cols], preferred_element_type=F32)
            for k in range(SPREAD):
                normed[pl.ds(pl.multiple_of(k * 128 + r * QUART, QUART), QUART), cols] = block[
                    k * QUART:(k + 1) * QUART].astype(BF16)
            col = col + jnp.sum(block * block, axis=1, keepdims=True)
        sq_own[r] = jnp.broadcast_to(jnp.sum(jnp.where(eye, col, 0.0), axis=0, keepdims=True), (8, 128))
        return c

    lax.fori_loop(0, ROWS_G, turn_rows, 0)

    def sq_copy(d):
        return pltpu.make_async_remote_copy(
            src_ref=sq_own, dst_ref=sq_got.at[3 - d], send_sem=sqs.at[d - 1], recv_sem=sqr.at[3 - d],
            device_id=(dp, wrap(t + d, 4)), device_id_type=MESH)

    for d in (1, 2, 3):
        sq_copy(d).start()

    gath_w.after_z()
    for d in (1, 2, 3):
        sq_copy(d).wait()

    def norm_rows(r, c):
        total = sq_own[r] + sq_got[0, r] + sq_got[1, r] + sq_got[2, r]
        scale = lax.rsqrt(total[0:1] / (width * TENSOR) + epsilon)
        col = jnp.sum(jnp.where(eye, scale, 0.0), axis=1, keepdims=True)
        for k in range(SPREAD):
            rows = pl.ds(pl.multiple_of(k * 128 + r * QUART, QUART), QUART)
            block = normed[rows, :].astype(F32) * col[k * QUART:(k + 1) * QUART] * gain_ref[...].astype(F32)
            normed[rows, :] = block.astype(BF16)
        return c

    lax.fori_loop(0, ROWS_G, norm_rows, 0)

    for i in (1, 2, 3):
        gath_w.after_first(i)
    gath_h.after_z()
    for i in range(4):
        gath_w.after_second(i)
    for i in (1, 2, 3):
        gath_h.after_first(i)
    for i in range(4):
        gath_w.after_onward(i)
    gath_w.after_across()

    def direction(k):
        return 1 if k >= 2 else -1

    def project(owner, row0, rows):
        zl = lax.div(owner, 2)

        def tile(y_lo, c):
            y = lax.rem(owner, 2) * 2 + y_lo
            wa = gw[0, y, :, zl].reshape(256, half_w)
            wb = gw[1, :, y, zl].reshape(256, half_w)
            res = dot_nt(normed[row0:row0 + rows, :half_w], wa)
            res = res + dot_nt(normed[row0:row0 + rows, half_w:], wb)
            pacc[row0:row0 + rows, pl.ds(pl.multiple_of(y_lo * 256, 256), 256)] = res
            return c

        lax.fori_loop(0, 2, tile, 0)

    def rs_copy(k, step):
        return pltpu.make_async_remote_copy(
            src_ref=rs_send.at[k, step], dst_ref=rs_recv.at[k, step], send_sem=rss.at[k, step],
            recv_sem=rsr.at[k, step], device_id=(dp, wrap(t + direction(k), 4)), device_id_type=MESH)

    def rot_copy(k):
        rows = scored_ref.at[pl.ds(k * 128, 128), :]
        return pltpu.make_async_remote_copy(
            src_ref=rs_send.at[k, 3], dst_ref=rows, send_sem=rot_s.at[k], recv_sem=rot_r.at[k],
            device_id=(lax.rem(dp + k, groups), t), device_id_type=MESH)

    def project_step(step):
        if step == 1:
            project(wrap(t + 2, 4), 0, 512)
        elif step == 3:
            project(t, 0, 512)
        else:
            project(wrap(t + 1 + step, 4), 0, 256)
            project(wrap(t - 1 - step, 4), 256, 256)

    def pass_step(step):
        for k in (3, 1, 2, 0):
            rows = slice(k * 128, (k + 1) * 128)
            total = pacc[rows, :]
            if step:
                rs_copy(k, step - 1).wait_recv()
                total = total + rs_recv[k, step - 1].astype(F32)
            if step == 3 and k == 0:
                scored_ref[rows, :] = total.astype(BF16)
                continue
            rs_send[k, step] = total.astype(BF16)
            if step < 3:
                rs_copy(k, step).start()
            else:
                rot_copy(k).start()

    project_step(0)
    pass_step(0)
    for i in range(4):
        gath_h.after_second(i)
    project_step(1)
    pass_step(1)
    for i in range(4):
        gath_h.after_onward(i)
    project_step(2)
    gath_h.after_across()

    def decode_part(owner, y_lo):
        zl = lax.div(owner, 2)
        y = lax.rem(owner, 2) * 2 + y_lo
        ha = gh[0, y, :, zl].reshape(128, width)
        hb = gh[1, :, y, zl].reshape(128, width)
        return (jnp.dot(ha, outp_ref[0], preferred_element_type=F32)
                + jnp.dot(hb, outp_ref[1], preferred_element_type=F32))

    def decode_tiles(i, c):
        dacc[i] = decode_part(lax.div(i, 2), lax.rem(i, 2))
        return c

    lax.fori_loop(0, 8, decode_tiles, 0)

    def ds_copy(y_lo, step):
        return pltpu.make_async_remote_copy(
            src_ref=ds_send.at[y_lo, step], dst_ref=ds_recv.at[y_lo, step], send_sem=dss.at[y_lo, step],
            recv_sem=dsr.at[y_lo, step], device_id=(dp, wrap(t + (1 if y_lo else -1), 4)), device_id_type=MESH)

    def decode_step(step):
        for y_lo in range(2):
            owner = wrap(t - (1 + step) * (1 if y_lo else -1), 4)
            total = dacc[owner * 2 + y_lo]
            if step:
                ds_copy(y_lo, step - 1).wait_recv()
                total = total + ds_recv[y_lo, step - 1].astype(F32)
            if step < 3:
                ds_send[y_lo, step] = total.astype(BF16)
                ds_copy(y_lo, step).start()
            else:
                dfin[pl.ds(y_lo * 8, 8)] = total.astype(BF16).reshape(8, 16, 128)

    decode_step(0)
    pass_step(2)
    decode_step(1)
    decode_step(2)
    project_step(3)
    decode_step(3)

    def each_message(do_far, do_near):
        def one(i, c):
            d = lax.div(t, 2) * 32 + lax.rem(t, 2) * 16 + lax.rem(i, 16)
            dest_t = lax.div(i, 16)
            src = dfin.at[lax.rem(i, 16)]
            dst = dec_ref.at[:, pl.ds(pl.multiple_of(dp * 128, 128), 128)]
            near = jnp.logical_and(d == dp, dest_t == t)

            @pl.when(near)
            def _():
                if do_near:
                    do_near(pltpu.make_async_copy(src, dst, out_r.at[0]))

            @pl.when(jnp.logical_not(near))
            def _():
                do_far(pltpu.make_async_remote_copy(
                    src_ref=src, dst_ref=dst, send_sem=out_s.at[i], recv_sem=out_r.at[0],
                    device_id=(d, dest_t), device_id_type=MESH))

            return c

        lax.fori_loop(0, 64, one, 0)

    each_message(lambda c: c.start(), lambda c: c.start())
    pass_step(3)
    for k in (3, 1, 2):
        rot_copy(k).wait()
    pltpu.make_async_copy(dec_ref, dec_ref, out_r.at[0]).wait()
    each_message(lambda c: c.wait_send(), None)
    for k in range(4):
        for step in range(3):
            rs_copy(k, step).wait_send()
    for y_lo in range(2):
        for step in range(3):
            ds_copy(y_lo, step).wait_send()
    gath_w.end()
    gath_h.end()


def exchange(pick, heads, out_proj, resp_act, gain, wt):
    width = wt.shape[1]
    vmem = pl.BlockSpec(memory_space=pltpu.VMEM)
    dma = pltpu.SemaphoreType.DMA
    return pl.pallas_call(
        kernel,
        out_shape=(
            jax.ShapeDtypeStruct((16, 8192), BF16),
            jax.ShapeDtypeStruct((512, 512), BF16),
        ),
        in_specs=[vmem] * 6,
        out_specs=(vmem, vmem),
        scratch_shapes=[
            pltpu.VMEM((2, 4, 4, 2, 2, 32, width // 2), BF16),
            pltpu.VMEM((2, 4, 4, 2, 2, 16, width), BF16),
            pltpu.VMEM((512, width), BF16),
            pltpu.VMEM((512, 512), F32),
            pltpu.VMEM((4, 4, 128, 512), BF16),
            pltpu.VMEM((4, 3, 128, 512), BF16),
            pltpu.VMEM((8, 128, 128), F32),
            pltpu.VMEM((2, 3, 128, 128), BF16),
            pltpu.VMEM((2, 3, 128, 128), BF16),
            pltpu.VMEM((16, 16, 128), BF16),
            pltpu.VMEM((4, 8, 128), F32),
            pltpu.VMEM((3, 4, 8, 128), F32),
            dma((2, 32)), dma((2, 32)), dma((2,)),
            dma((2, 32)), dma((2, 32)), dma((2,)),
            dma((4, 3)), dma((4, 3)), dma((2, 3)), dma((2, 3)),
            dma((3,)), dma((3,)), dma((4,)), dma((4,)), dma((64,)), dma((1,)),
        ],
        compiler_params=pltpu.CompilerParams(
            collective_id=0, has_side_effects=True, vmem_limit_bytes=56 * 1024 * 1024),
    )(pick, heads, out_proj, resp_act, gain, wt)


def attend(queries, fresh_kv, kv_cache, cache_len):
    steps, layers, rows, width = queries.shape
    cache = kv_cache.shape[2]
    kvs = kv_cache.shape[-1] // HEAD
    group = width // (kvs * HEAD)
    scale = 1.0 / math.sqrt(HEAD)
    q = queries.reshape(steps, layers, rows, kvs, group, HEAD)
    c = kv_cache.reshape(layers, rows, cache, 2, kvs, HEAD)
    f = fresh_kv.reshape(steps, layers, rows, 2, kvs, HEAD)
    cs = jnp.einsum("slrkgd,lrpkd->lrksgp", q, c[:, :, :, 0], preferred_element_type=jnp.float32) * scale
    fs = jnp.einsum("slrkgd,ulrkd->lrksgu", q, f[:, :, :, 0], preferred_element_type=jnp.float32) * scale
    valid = jnp.arange(cache, dtype=jnp.int32)[None, :] < cache_len[:, None]
    cs = jnp.where(valid[None, :, None, None, None, :], cs, masked_score)
    order = jnp.arange(steps, dtype=jnp.int32)
    seen = order[None, :] <= order[:, None]
    fs = jnp.where(seen[None, None, None, :, None, :], fs, masked_score)
    peak = jnp.maximum(cs.max(-1), fs.max(-1))[..., None]
    ce = jnp.exp(cs - peak)
    fe = jnp.exp(fs - peak)
    total = ce.sum(-1, keepdims=True) + fe.sum(-1, keepdims=True)
    cw = (ce / total).astype(jnp.bfloat16)
    fw = (fe / total).astype(jnp.bfloat16)
    out = jnp.einsum("lrksgp,lrpkd->srlkgd", cw, c[:, :, :, 1], preferred_element_type=jnp.float32)
    out = out + jnp.einsum("lrksgu,ulrkd->srlkgd", fw, f[:, :, :, 1], preferred_element_type=jnp.float32)
    return out.astype(jnp.bfloat16).reshape(steps * rows, layers * width)


def pick_matrix(finished, resp_len, start_shard):
    place = jnp.arange(SPREAD * QUART, dtype=jnp.int32)
    block = jnp.mod(place[None, :] // QUART - start_shard[:, None], SPREAD)
    source = block * QUART + place[None, :] % QUART
    live = (finished[:, None] == 1) & (source < resp_len[:, None])
    return ((source[:, :, None] == place) & live[:, :, None]).astype(BF16)


def shards(
    queries,
    fresh_kv,
    kv_cache,
    cache_len,
    out_proj,
    finished,
    resp_len,
    start_shard,
    resp_act,
    reward_gain,
    reward_weight,
):
    steps, layers, rows, width = queries.shape
    heads = attend(queries, fresh_kv, kv_cache, cache_len)
    pick = pick_matrix(finished, resp_len, start_shard)
    dec, scored = exchange(
        pick, heads, out_proj, resp_act, reward_gain.reshape(1, -1), reward_weight.T
    )
    return dec.reshape(steps, rows, -1), scored


def solution(mesh):
    return jax.shard_map(
        shards,
        mesh=mesh,
        in_specs=(
            P(None, None, "dp", "tensor"),
            P(None, None, "dp", None, "tensor"),
            P(None, "dp", None, None, "tensor"),
            P("dp"),
            P(None, "tensor", "dp"),
            P("dp"),
            P("dp"),
            P("dp"),
            P("dp", None, "tensor"),
            P("tensor"),
            P("tensor", "dp"),
        ),
        out_specs=(P(None, "dp", None), P("dp", "tensor")),
        check_vma=False,
    )
```

```python
import functools
import math

import jax
import jax.numpy as jnp
from jax import lax
from jax.experimental import pallas as pl
from jax.experimental.pallas import tpu as pltpu
from jax.sharding import PartitionSpec as P

HEAD = 128
SPREAD = 4
QUART = 32
ROWS_G = 4
TENSOR = 4

epsilon = 1e-05
masked_score = -1e30

MESH = pl.DeviceIdType.MESH
STEP_OFF = (0, 1, -1, 2)
BACK = {1: 2, -1: 1, 2: 3}
F32 = jnp.float32
BF16 = jnp.bfloat16


def wrap(v, n):
    return lax.rem(v + 2 * n, n)


class Place:
    def __init__(self):
        self.dp = lax.axis_index("dp")
        self.t = lax.axis_index("tensor")
        self.core = lax.rem(self.dp, 2)
        self.x = lax.rem(self.dp // 2, 4)
        self.y = lax.rem(self.dp // 8, 4)
        self.zl = self.dp // 32

    def at(self, zl, y, x, core):
        return (((zl * 4 + y) * 4 + x) * 2 + core, self.t)


class Gather:
    def __init__(self, place, own, out, send, recv, local):
        self.p, self.own, self.out, self.send, self.recv, self.local = place, own, out, send, recv, local

    def ring(self, h):
        return (self.p.y, self.p.x) if h == 0 else (self.p.x, self.p.y)

    def dev(self, h, s, f, zl=None, core=None):
        p = self.p
        zl = p.zl if zl is None else zl
        core = p.core if core is None else core
        return p.at(zl, s, f, core) if h == 0 else p.at(zl, f, s, core)

    def unit(self, h, j, core=None):
        s, f = self.ring(h)
        s = wrap(s + STEP_OFF[j // 4], 4)
        f = wrap(f + STEP_OFF[j % 4], 4)
        return self.out.at[h, s, f, :, self.p.core if core is None else core]

    def copy(self, h, src, dst, send, recv, dev):
        return pltpu.make_async_remote_copy(
            src_ref=src, dst_ref=dst, send_sem=self.send.at[h, send], recv_sem=self.recv.at[h, recv],
            device_id=dev, device_id_type=MESH)

    def z_copy(self, h):
        s, f = self.ring(h)
        return self.copy(h, self.own(h), self.out.at[h, s, f, self.p.zl, self.p.core], 0, 0,
                         self.dev(h, s, f, zl=1 - self.p.zl))

    def own_copy(self, h):
        s, f = self.ring(h)
        return pltpu.make_async_copy(self.own(h), self.out.at[h, s, f, self.p.zl, self.p.core], self.local.at[h])

    def start(self):
        for h in range(2):
            self.z_copy(h).start()
            self.own_copy(h).start()

    def first(self, h, i):
        s, f = self.ring(h)
        u = self.unit(h, 0)
        return self.copy(h, u, u, i, BACK[STEP_OFF[i]], self.dev(h, s, wrap(f + STEP_OFF[i], 4)))

    def second(self, h, i, right):
        s, f = self.ring(h)
        u = self.unit(h, i)
        step = 1 if right else -1
        base = 8 if right else 4
        return self.copy(h, u, u, base + i, base + i, self.dev(h, wrap(s + step, 4), f))

    def onward(self, h, i):
        s, f = self.ring(h)
        u = self.unit(h, (8 if i < 2 else 4) + i)
        return self.copy(h, u, u, 12 + i, 12 + i, self.dev(h, wrap(s + (1 if i < 2 else -1), 4), f))

    def across(self, h, j):
        s, f = self.ring(h)
        u = self.unit(h, j)
        return self.copy(h, u, u, 16 + j, 16 + j, self.dev(h, s, f, core=1 - self.p.core))

    def arrived(self, h, j):
        u = self.unit(h, j)
        self.copy(h, u, u, j, j, self.dev(h, *self.ring(h), core=1 - self.p.core)).wait_recv()

    def after_z(self):
        for h in range(2):
            s, f = self.ring(h)
            u = self.out.at[h, s, f, 1 - self.p.zl, self.p.core]
            self.copy(h, u, u, 0, 0, self.dev(h, s, f, zl=1 - self.p.zl)).wait_recv()
            self.own_copy(h).wait()
            for i in (1, 2, 3):
                self.first(h, i).start()
            for right in (True, False):
                self.second(h, 0, right).start()
            self.across(h, 0).start()

    def after_first(self, i):
        for h in range(2):
            self.arrived(h, i)
            for right in (True, False):
                self.second(h, i, right).start()
            self.across(h, i).start()

    def after_second(self, i):
        for h in range(2):
            for j in ((8 + i, 4 + i) if i < 2 else (4 + i, 8 + i)):
                self.arrived(h, j)
                if j == (8 if i < 2 else 4) + i:
                    self.onward(h, i).start()
                self.across(h, j).start()

    def after_onward(self, i):
        for h in range(2):
            self.arrived(h, 12 + i)
            self.across(h, 12 + i).start()

    def after_across(self):
        for h in range(2):
            for j in range(16):
                u = self.unit(h, j, core=1 - self.p.core)
                self.copy(h, u, u, 16 + j, 16 + j, self.dev(h, *self.ring(h), core=1 - self.p.core)).wait_recv()

    def end(self):
        for h in range(2):
            self.z_copy(h).wait_send()
            for i in (1, 2, 3):
                self.first(h, i).wait_send()
            for i in range(4):
                self.second(h, i, True).wait_send()
                self.second(h, i, False).wait_send()
                self.onward(h, i).wait_send()
            for j in range(16):
                self.across(h, j).wait_send()


def eye_mask():
    return lax.broadcasted_iota(jnp.int32, (128, 128), 0) == lax.broadcasted_iota(jnp.int32, (128, 128), 1)


def dot_nt(a, b):
    return lax.dot_general(a, b, (((1,), (1,)), ((), ())), preferred_element_type=F32)


def kernel(
    meta_ref, q_ref, fresh_ref, gain_ref, kv_hbm, outp_hbm, resp_hbm, wt_ref,
    dec_ref, scored_ref,
    kv_ref, outp_ref, resp_ref, q_rows, heads_ref, by_row, gw, gh, normed, pacc, rs_send, rs_recv, dacc, ds_send, ds_recv, dfin, sq_own, sq_got,
    w_send, w_recv, w_local, h_send, h_recv, h_local,
    rss, rsr, dss, dsr, sqs, sqr, rot_s, rot_r, out_s, out_r, in_s,
):
    p = Place()
    dp, t = p.dp, p.t
    groups = 64
    width = wt_ref.shape[1]
    half_w = width // 2
    is_self = lax.div(dp, 16) == t

    resp_in = pltpu.make_async_copy(resp_hbm, resp_ref, in_s.at[0])
    kv_in = pltpu.make_async_copy(kv_hbm, kv_ref, in_s.at[1])
    outp_in = pltpu.make_async_copy(outp_hbm, outp_ref, in_s.at[2])
    resp_in.start()
    kv_in.start()
    outp_in.start()

    barrier = pltpu.get_barrier_semaphore()

    def greet(dev):
        pl.semaphore_signal(barrier, inc=1, device_id=dev, device_id_type=MESH)

    greet(p.at(1 - p.zl, p.y, p.x, p.core))
    greet(p.at(p.zl, p.y, p.x, 1 - p.core))
    for d in (1, 2, 3):
        greet(p.at(p.zl, p.y, wrap(p.x + d, 4), p.core))
        greet(p.at(p.zl, wrap(p.y + d, 4), p.x, p.core))
        greet((dp, wrap(t + d, 4)))
        greet((wrap(dp - d, groups), t))

    def greet_source(d, c):
        src_t = lax.div(dp, 16)

        @pl.when(jnp.logical_not(jnp.logical_and(d == dp, src_t == t)))
        def _():
            greet((d, src_t))

        return c

    lax.fori_loop(0, groups, greet_source, 0)
    pl.semaphore_wait(barrier, 14 + groups - is_self.astype(jnp.int32))

    gath_w = Gather(p, lambda h: wt_ref.at[:, pl.ds(h * half_w, half_w)], gw, w_send, w_recv, w_local)
    gath_h = Gather(p, lambda h: heads_ref.at[:, pl.ds(h * width, width)], gh, h_send, h_recv, h_local)
    gath_w.start()

    eye = eye_mask()

    row_no = lax.broadcasted_iota(jnp.int32, (128, 128), 0)
    col_no = lax.broadcasted_iota(jnp.int32, (128, 128), 1)

    def turn_rows(r, c):
        block_no = jnp.bitwise_and(row_no // QUART - meta_ref[3, pl.ds(r, 1), :], SPREAD - 1)
        source = block_no * QUART + jnp.bitwise_and(row_no, QUART - 1)
        live = jnp.logical_and(source < meta_ref[2, pl.ds(r, 1), :], meta_ref[1, pl.ds(r, 1), :] == 1)
        pick = jnp.where(jnp.logical_and(source == col_no, live), 1.0, 0.0).astype(BF16)
        col = jnp.zeros((128, 1), F32)
        for part in range(4):
            cols = slice(part * (width // 4), (part + 1) * (width // 4))
            block = jnp.dot(pick, resp_ref[r, :, cols], preferred_element_type=F32)
            for k in range(SPREAD):
                normed[pl.ds(pl.multiple_of(k * 128 + r * QUART, QUART), QUART), cols] = block[
                    k * QUART:(k + 1) * QUART].astype(BF16)
            col = col + jnp.sum(block * block, axis=1, keepdims=True)
        sq_own[r] = jnp.broadcast_to(jnp.sum(jnp.where(eye, col, 0.0), axis=0, keepdims=True), (8, 128))
        return c

    resp_in.wait()
    lax.fori_loop(0, ROWS_G, turn_rows, 0)

    def sq_copy(d):
        return pltpu.make_async_remote_copy(
            src_ref=sq_own, dst_ref=sq_got.at[3 - d], send_sem=sqs.at[d - 1], recv_sem=sqr.at[3 - d],
            device_id=(dp, wrap(t + d, 4)), device_id_type=MESH)

    for d in (1, 2, 3):
        sq_copy(d).start()

    gain = jnp.concatenate([gain_ref[i:i + 1, :].astype(F32) for i in range(width // 128)], axis=1)

    def norm_rows(r, c):
        total = sq_own[r] + sq_got[0, r] + sq_got[1, r] + sq_got[2, r]
        scale = lax.rsqrt(total[0:1] / (width * TENSOR) + epsilon)
        col = jnp.sum(jnp.where(eye, scale, 0.0), axis=1, keepdims=True)
        for k in range(SPREAD):
            rows = pl.ds(pl.multiple_of(k * 128 + r * QUART, QUART), QUART)
            block = normed[rows, :].astype(F32) * col[k * QUART:(k + 1) * QUART] * gain
            normed[rows, :] = block.astype(BF16)
        return c

    scale_q = 1.0 / math.sqrt(HEAD)
    fresh_no = lax.broadcasted_iota(jnp.int32, (32, 8), 1)
    seen = jnp.logical_and(fresh_no % 2 == 0, fresh_no // 2 <= lax.broadcasted_iota(jnp.int32, (32, 8), 0) // 8)
    cache_no = lax.broadcasted_iota(jnp.int32, (1, 1024), 1)

    def order_queries(layer):
        for head in range(2):
            for step in range(4):
                for g in range(8):
                    begin = (head * 8 + g) * HEAD
                    q_rows[layer * 2 + head, pl.ds(step * 8 + g, 4, stride=32), :] = q_ref[
                        step, layer, :, begin:begin + HEAD].astype(F32)

    def attend_row(layer, head, r):
        q = q_rows[layer * 2 + head, r * 32:(r + 1) * 32, :]
        both = kv_ref[layer, r, :, :, head * HEAD:(head + 1) * HEAD].reshape(1024, HEAD)
        new = fresh_ref[:, layer, r, :, head * HEAD:(head + 1) * HEAD].astype(F32).reshape(8, HEAD)
        valid = jnp.logical_and(cache_no % 2 == 0, cache_no < 2 * meta_ref[0, r:r + 1, 0:1])
        cs = jnp.where(valid, dot_nt(q.astype(BF16), both) * scale_q, masked_score)
        fs = jnp.where(seen, dot_nt(q, new) * scale_q, masked_score)
        peak = jnp.maximum(jnp.max(cs, axis=1, keepdims=True), jnp.max(fs, axis=1, keepdims=True))
        ce = jnp.exp(cs - peak)
        fe = jnp.exp(fs - peak)
        total = jnp.sum(ce, axis=1, keepdims=True) + jnp.sum(fe, axis=1, keepdims=True)
        cw = pltpu.roll(ce / total, 1, 1).astype(BF16)
        fw = (fe / total).astype(BF16).astype(F32)
        res = jnp.dot(cw, both, preferred_element_type=F32)
        res = res + jnp.dot(fw, pltpu.roll(new, 7, 0), preferred_element_type=F32)
        for step in range(4):
            by_row[(step * 4 + r) * 8:(step * 4 + r + 1) * 8, :] = res[step * 8:(step + 1) * 8]

    def attend_end(layer, head):
        for g in range(8):
            begin = layer * width + head * 8 * HEAD + g * HEAD
            heads_ref[:, begin:begin + HEAD] = by_row[pl.ds(g, 16, stride=8), :].astype(BF16)

    order_queries(0)
    order_queries(1)
    gath_w.after_z()
    kv_in.wait()
    events = {
        1: lambda: gath_w.after_first(1),
        2: lambda: gath_w.after_first(2),
        4: lambda: gath_w.after_first(3),
        6: lambda: gath_w.after_second(0),
        8: lambda: gath_w.after_second(1),
        10: lambda: gath_w.after_second(2),
        12: lambda: gath_w.after_second(3),
        14: lambda: gath_w.after_onward(0),
    }
    for u in range(16):
        attend_row(u // 8, (u // 4) % 2, u % 4)
        if u % 4 == 3:
            attend_end(u // 8, (u // 4) % 2)
        if u in events:
            events[u]()
    gath_h.start()
    for d in (1, 2, 3):
        sq_copy(d).wait()
    lax.fori_loop(0, ROWS_G, norm_rows, 0)
    gath_h.after_z()
    for i in (1, 2, 3):
        gath_w.after_onward(i)
    gath_w.after_across()

    def direction(k):
        return 1 if k >= 2 else -1

    def project(owner, row0, rows):
        zl = lax.div(owner, 2)

        def tile(y_lo, c):
            y = lax.rem(owner, 2) * 2 + y_lo
            wa = gw[0, y, :, zl].reshape(256, half_w)
            wb = gw[1, :, y, zl].reshape(256, half_w)
            res = dot_nt(normed[row0:row0 + rows, :half_w], wa)
            res = res + dot_nt(normed[row0:row0 + rows, half_w:], wb)
            pacc[row0:row0 + rows, pl.ds(pl.multiple_of(y_lo * 256, 256), 256)] = res
            return c

        lax.fori_loop(0, 2, tile, 0)

    def rs_copy(k, step):
        return pltpu.make_async_remote_copy(
            src_ref=rs_send.at[k, step], dst_ref=rs_recv.at[k, step], send_sem=rss.at[k, step],
            recv_sem=rsr.at[k, step], device_id=(dp, wrap(t + direction(k), 4)), device_id_type=MESH)

    def rot_copy(k):
        rows = scored_ref.at[pl.ds(k * 128, 128), :]
        return pltpu.make_async_remote_copy(
            src_ref=rs_send.at[k, 3], dst_ref=rows, send_sem=rot_s.at[k], recv_sem=rot_r.at[k],
            device_id=(lax.rem(dp + k, groups), t), device_id_type=MESH)

    def project_step(step):
        if step == 1:
            project(wrap(t + 2, 4), 0, 512)
        elif step == 3:
            project(t, 0, 512)
        else:
            project(wrap(t + 1 + step, 4), 0, 256)
            project(wrap(t - 1 - step, 4), 256, 256)

    def pass_step(step):
        for k in (3, 1, 2, 0):
            rows = slice(k * 128, (k + 1) * 128)
            total = pacc[rows, :]
            if step:
                rs_copy(k, step - 1).wait_recv()
                total = total + rs_recv[k, step - 1].astype(F32)
            if step == 3 and k == 0:
                scored_ref[rows, :] = total.astype(BF16)
                continue
            rs_send[k, step] = total.astype(BF16)
            if step < 3:
                rs_copy(k, step).start()
            else:
                rot_copy(k).start()

    project_step(0)
    pass_step(0)
    for i in (1, 2, 3):
        gath_h.after_first(i)
    for i in range(2):
        gath_h.after_second(i)
    project_step(1)
    pass_step(1)
    for i in range(2, 4):
        gath_h.after_second(i)
    for i in range(4):
        gath_h.after_onward(i)
    project_step(2)
    gath_h.after_across()

    def decode_part(owner, y_lo):
        zl = lax.div(owner, 2)
        y = lax.rem(owner, 2) * 2 + y_lo
        ha = gh[0, y, :, zl].reshape(128, width)
        hb = gh[1, :, y, zl].reshape(128, width)
        return (jnp.dot(ha, outp_ref[0], preferred_element_type=F32)
                + jnp.dot(hb, outp_ref[1], preferred_element_type=F32))

    def ds_copy(d):
        return pltpu.make_async_remote_copy(
            src_ref=ds_send.at[d - 1], dst_ref=ds_recv.at[3 - d], send_sem=dss.at[d - 1], recv_sem=dsr.at[3 - d],
            device_id=(dp, wrap(t + d, 4)), device_id_type=MESH)

    outp_in.wait()
    for d in (2, 1, 3):
        for y_lo in range(2):
            ds_send[d - 1, y_lo * 128:(y_lo + 1) * 128] = decode_part(wrap(t + d, 4), y_lo).astype(BF16)
        ds_copy(d).start()
    for y_lo in range(2):
        dacc[y_lo] = decode_part(t, y_lo)
    pass_step(2)
    project_step(3)
    for d in (1, 2, 3):
        ds_copy(d).wait_recv()
    for y_lo in range(2):
        total = dacc[y_lo]
        for d in range(3):
            total = total + ds_recv[d, y_lo * 128:(y_lo + 1) * 128].astype(F32)
        dfin[pl.ds(y_lo * 8, 8)] = total.astype(BF16).reshape(8, 16, 128)

    def each_message(do_far, do_near):
        def one(i, c):
            d = lax.div(t, 2) * 32 + lax.rem(t, 2) * 16 + lax.rem(i, 16)
            dest_t = lax.div(i, 16)
            src = dfin.at[lax.rem(i, 16)]
            dst = dec_ref.at[:, pl.ds(pl.multiple_of(dp * 128, 128), 128)]
            near = jnp.logical_and(d == dp, dest_t == t)

            @pl.when(near)
            def _():
                if do_near:
                    do_near(pltpu.make_async_copy(src, dst, out_r.at[0]))

            @pl.when(jnp.logical_not(near))
            def _():
                do_far(pltpu.make_async_remote_copy(
                    src_ref=src, dst_ref=dst, send_sem=out_s.at[i], recv_sem=out_r.at[0],
                    device_id=(d, dest_t), device_id_type=MESH))

            return c

        lax.fori_loop(0, 64, one, 0)

    each_message(lambda c: c.start(), lambda c: c.start())
    pass_step(3)
    for k in (3, 1, 2):
        rot_copy(k).wait()
    pltpu.make_async_copy(dec_ref, dec_ref, out_r.at[0]).wait()
    each_message(lambda c: c.wait_send(), None)
    for k in range(4):
        for step in range(3):
            rs_copy(k, step).wait_send()
    for d in (1, 2, 3):
        ds_copy(d).wait_send()
    gath_w.end()
    gath_h.end()


def exchange(meta, q, fresh, gain, kv_cache, out_proj, resp_act, wt):
    width = wt.shape[1]
    vmem = pl.BlockSpec(memory_space=pltpu.VMEM)
    dma = pltpu.SemaphoreType.DMA
    return pl.pallas_call(
        kernel,
        out_shape=(
            jax.ShapeDtypeStruct((16, 8192), BF16),
            jax.ShapeDtypeStruct((512, 512), BF16),
        ),
        in_specs=[vmem] * 4 + [pl.BlockSpec(memory_space=pl.ANY)] * 4,
        out_specs=(vmem, vmem),
        scratch_shapes=[
            pltpu.VMEM(kv_cache.shape, BF16),
            pltpu.VMEM(out_proj.shape, BF16),
            pltpu.VMEM(resp_act.shape, BF16),
            pltpu.VMEM((4, 128, 128), F32),
            pltpu.VMEM((16, 2 * width), BF16),
            pltpu.VMEM((128, 128), F32),
            pltpu.VMEM((2, 4, 4, 2, 2, 32, width // 2), BF16),
            pltpu.VMEM((2, 4, 4, 2, 2, 16, width), BF16),
            pltpu.VMEM((512, width), BF16),
            pltpu.VMEM((512, 512), F32),
            pltpu.VMEM((4, 4, 128, 512), BF16),
            pltpu.VMEM((4, 3, 128, 512), BF16),
            pltpu.VMEM((2, 128, 128), F32),
            pltpu.VMEM((3, 256, 128), BF16),
            pltpu.VMEM((3, 256, 128), BF16),
            pltpu.VMEM((16, 16, 128), BF16),
            pltpu.VMEM((4, 8, 128), F32),
            pltpu.VMEM((3, 4, 8, 128), F32),
            dma((2, 32)), dma((2, 32)), dma((2,)),
            dma((2, 32)), dma((2, 32)), dma((2,)),
            dma((4, 3)), dma((4, 3)), dma((3,)), dma((3,)),
            dma((3,)), dma((3,)), dma((4,)), dma((4,)), dma((64,)), dma((1,)), dma((3,)),
        ],
        compiler_params=pltpu.CompilerParams(
            collective_id=0, has_side_effects=True, vmem_limit_bytes=56 * 1024 * 1024),
    )(meta, q, fresh, gain, kv_cache, out_proj, resp_act, wt)


def shards(
    queries,
    fresh_kv,
    kv_cache,
    cache_len,
    out_proj,
    finished,
    resp_len,
    start_shard,
    resp_act,
    reward_gain,
    reward_weight,
):
    steps, layers, rows, width = queries.shape
    meta = jnp.stack([cache_len, finished, resp_len, start_shard])
    meta = jnp.broadcast_to(meta[:, :, None], (4, rows, 128))
    dec, scored = exchange(
        meta, queries, fresh_kv, reward_gain.reshape(-1, 128), kv_cache, out_proj, resp_act, reward_weight.T
    )
    return dec.reshape(steps, rows, -1), scored


def solution(mesh):
    return jax.shard_map(
        shards,
        mesh=mesh,
        in_specs=(
            P(None, None, "dp", "tensor"),
            P(None, None, "dp", None, "tensor"),
            P(None, "dp", None, None, "tensor"),
            P("dp"),
            P(None, "tensor", "dp"),
            P("dp"),
            P("dp"),
            P("dp"),
            P("dp", None, "tensor"),
            P("tensor"),
            P("tensor", "dp"),
        ),
        out_specs=(P(None, "dp", None), P("dp", "tensor")),
        check_vma=False,
    )
```

```python
import functools
import math

import jax
import jax.numpy as jnp
from jax import lax
from jax.experimental import pallas as pl
from jax.experimental.pallas import tpu as pltpu
from jax.sharding import PartitionSpec as P

HEAD = 128
SPREAD = 4
QUART = 32
ROWS_G = 4
TENSOR = 4

epsilon = 1e-05
masked_score = -1e30

MESH = pl.DeviceIdType.MESH
STEP_OFF = (0, 1, -1, 2)
BACK = {1: 2, -1: 1}
Z, NEAR, FAR, SECOND, ONWARD, ACROSS = range(6)
F32 = jnp.float32
BF16 = jnp.bfloat16


def wrap(v, n):
    return lax.rem(v + 2 * n, n)


class Place:
    def __init__(self):
        self.dp = lax.axis_index("dp")
        self.t = lax.axis_index("tensor")
        self.core = lax.rem(self.dp, 2)
        self.x = lax.rem(self.dp // 2, 4)
        self.y = lax.rem(self.dp // 8, 4)
        self.zl = self.dp // 32

    def at(self, zl, y, x, core):
        return (((zl * 4 + y) * 4 + x) * 2 + core, self.t)


class Gather:
    def __init__(self, place, own, out, send, recv, cross, local):
        self.p, self.own, self.out, self.send, self.recv = place, own, out, send, recv
        self.cross, self.local = cross, local

    def ring(self, h):
        return (self.p.y, self.p.x) if h == 0 else (self.p.x, self.p.y)

    def dev(self, h, s, f, zl=None, core=None):
        p = self.p
        zl = p.zl if zl is None else zl
        core = p.core if core is None else core
        return p.at(zl, s, f, core) if h == 0 else p.at(zl, f, s, core)

    def unit(self, h, j, core=None):
        s, f = self.ring(h)
        s = wrap(s + STEP_OFF[j // 4], 4)
        f = wrap(f + STEP_OFF[j % 4], 4)
        return self.out.at[h, s, f, :, self.p.core if core is None else core]

    def copy(self, h, src, dst, send, recv, dev):
        return pltpu.make_async_remote_copy(
            src_ref=src, dst_ref=dst, send_sem=self.send.at[send],
            recv_sem=self.cross.at[0] if send == ACROSS else self.recv.at[h, recv],
            device_id=dev, device_id_type=MESH)

    def z_copy(self, h):
        s, f = self.ring(h)
        return self.copy(h, self.own(h), self.out.at[h, s, f, self.p.zl, self.p.core], Z, 0,
                         self.dev(h, s, f, zl=1 - self.p.zl))

    def own_copy(self, h):
        s, f = self.ring(h)
        return pltpu.make_async_copy(self.own(h), self.out.at[h, s, f, self.p.zl, self.p.core], self.local.at[h])

    def start(self):
        for h in range(2):
            self.z_copy(h).start()
            self.own_copy(h).start()

    def first(self, h, i):
        s, f = self.ring(h)
        u = self.unit(h, 0)
        return self.copy(h, u, u, NEAR, BACK[STEP_OFF[i]], self.dev(h, s, wrap(f + STEP_OFF[i], 4)))

    def far(self, h, i):
        s, f = self.ring(h)
        u = self.out.at[h, s, wrap(f + STEP_OFF[i], 4), i - 1, self.p.core]
        return self.copy(h, u, u, FAR, 3 if i == 1 else 16, self.dev(h, s, wrap(f - STEP_OFF[i], 4)))

    def second(self, h, i, right):
        s, f = self.ring(h)
        u = self.unit(h, i)
        return self.copy(h, u, u, SECOND, (8 if right else 4) + i, self.dev(h, wrap(s + (1 if right else -1), 4), f))

    def onward(self, h, i):
        s, f = self.ring(h)
        u = self.unit(h, (8 if i < 2 else 4) + i)
        return self.copy(h, u, u, ONWARD, 12 + i, self.dev(h, wrap(s + (1 if i < 2 else -1), 4), f))

    def across(self, h, j):
        s, f = self.ring(h)
        u = self.unit(h, j)
        return self.copy(h, u, u, ACROSS, 0, self.dev(h, s, f, core=1 - self.p.core))

    def wait_for(self, h, ref, recv):
        pltpu.make_async_copy(ref, ref, self.recv.at[h, recv]).wait()

    def arrived(self, h, j):
        self.wait_for(h, self.unit(h, j), j)

    def after_z(self):
        for h in range(2):
            s, f = self.ring(h)
            self.wait_for(h, self.out.at[h, s, f, 1 - self.p.zl, self.p.core], 0)
            self.own_copy(h).wait()
            for i in (1, 2):
                self.first(h, i).start()
            for right in (True, False):
                self.second(h, 0, right).start()
            self.across(h, 0).start()

    def after_first(self, i):
        for h in range(2):
            if i < 3:
                self.arrived(h, i)
                self.far(h, i).start()
            else:
                s, f = self.ring(h)
                for zl in range(2):
                    self.wait_for(h, self.out.at[h, s, wrap(f + 2, 4), zl, self.p.core], 16 if zl else 3)
            for right in (True, False):
                self.second(h, i, right).start()
            self.across(h, i).start()

    def after_second(self, i):
        for h in range(2):
            for j in ((8 + i, 4 + i) if i < 2 else (4 + i, 8 + i)):
                self.arrived(h, j)
                if j == (8 if i < 2 else 4) + i:
                    self.onward(h, i).start()
                self.across(h, j).start()

    def after_onward(self, i):
        for h in range(2):
            self.arrived(h, 12 + i)
            self.across(h, 12 + i).start()

    def after_across(self):
        u = self.out.at[:, :, :, :, 1 - self.p.core]
        pltpu.make_async_copy(u, u, self.cross.at[0]).wait()

    def end(self):
        sent = {
            Z: self.out.at[:, 0, 0, 0, 0],
            NEAR: self.out.at[:, 0, pl.ds(0, 2), :, 0],
            FAR: self.out.at[:, 0, 0, :, 0],
            SECOND: self.out.at[:, pl.ds(0, 2), :, :, 0],
            ONWARD: self.out.at[:, 0, :, :, 0],
            ACROSS: self.out.at[:, :, :, :, 0],
        }
        for kind, ref in sent.items():
            pltpu.make_async_copy(ref, ref, self.send.at[kind]).wait()


def eye_mask():
    return lax.broadcasted_iota(jnp.int32, (128, 128), 0) == lax.broadcasted_iota(jnp.int32, (128, 128), 1)


def dot_nt(a, b):
    return lax.dot_general(a, b, (((1,), (1,)), ((), ())), preferred_element_type=F32)


def kernel(
    meta_ref, q_ref, fresh_ref, gain_ref, kv_hbm, outp_hbm, resp_hbm, wt_ref,
    dec_ref, scored_ref,
    kv_ref, outp_ref, resp_ref, q_rows, heads_ref, by_row, gw, gh, normed, pacc, rs_send, rs_recv, dacc, ds_send, ds_recv, dfin, sq_own, sq_got,
    w_send, w_recv, w_cross, w_local, h_send, h_recv, h_cross, h_local,
    rss, rsr, dss, dsr, sqs, sqr, rot_s, rot_r, out_s, out_r, in_s,
):
    p = Place()
    dp, t = p.dp, p.t
    groups = 64
    width = wt_ref.shape[1]
    half_w = width // 2
    is_self = lax.div(dp, 16) == t

    def wait_all(ref, sem):
        pltpu.make_async_copy(ref, ref, sem.at[0]).wait()


    resp_in = pltpu.make_async_copy(resp_hbm, resp_ref, in_s.at[0])
    kv_in = pltpu.make_async_copy(kv_hbm, kv_ref, in_s.at[1])
    outp_in = pltpu.make_async_copy(outp_hbm, outp_ref, in_s.at[2])
    resp_in.start()
    kv_in.start()
    outp_in.start()

    barrier = pltpu.get_barrier_semaphore()

    def greet(dev):
        pl.semaphore_signal(barrier, inc=1, device_id=dev, device_id_type=MESH)

    greet(p.at(1 - p.zl, p.y, p.x, p.core))
    greet(p.at(p.zl, p.y, p.x, 1 - p.core))
    for d in (1, 2, 3):
        greet(p.at(p.zl, p.y, wrap(p.x + d, 4), p.core))
        greet(p.at(p.zl, wrap(p.y + d, 4), p.x, p.core))
        greet((dp, wrap(t + d, 4)))
        greet((wrap(dp - d, groups), t))

    pl.semaphore_wait(barrier, 14)

    gath_w = Gather(p, lambda h: wt_ref.at[:, pl.ds(h * half_w, half_w)], gw, w_send, w_recv, w_cross, w_local)
    gath_h = Gather(p, lambda h: heads_ref.at[:, pl.ds(h * width, width)], gh, h_send, h_recv, h_cross, h_local)
    gath_w.start()

    eye = eye_mask()

    row_no = lax.broadcasted_iota(jnp.int32, (128, 128), 0)
    col_no = lax.broadcasted_iota(jnp.int32, (128, 128), 1)

    def turn_rows(r, c):
        block_no = jnp.bitwise_and(row_no // QUART - meta_ref[3, pl.ds(r, 1), :], SPREAD - 1)
        source = block_no * QUART + jnp.bitwise_and(row_no, QUART - 1)
        live = jnp.logical_and(source < meta_ref[2, pl.ds(r, 1), :], meta_ref[1, pl.ds(r, 1), :] == 1)
        pick = jnp.where(jnp.logical_and(source == col_no, live), 1.0, 0.0).astype(BF16)
        col = jnp.zeros((128, 1), F32)
        for part in range(4):
            cols = slice(part * (width // 4), (part + 1) * (width // 4))
            block = jnp.dot(pick, resp_ref[r, :, cols], preferred_element_type=F32)
            for k in range(SPREAD):
                normed[pl.ds(pl.multiple_of(k * 128 + r * QUART, QUART), QUART), cols] = block[
                    k * QUART:(k + 1) * QUART].astype(BF16)
            col = col + jnp.sum(block * block, axis=1, keepdims=True)
        sq_own[r] = jnp.broadcast_to(jnp.sum(jnp.where(eye, col, 0.0), axis=0, keepdims=True), (8, 128))
        return c

    def sq_copy(d):
        return pltpu.make_async_remote_copy(
            src_ref=sq_own, dst_ref=sq_got.at[3 - d], send_sem=sqs.at[0], recv_sem=sqr.at[0],
            device_id=(dp, wrap(t + d, 4)), device_id_type=MESH)

    gain = jnp.concatenate([gain_ref[i:i + 1, :].astype(F32) for i in range(width // 128)], axis=1)

    def norm_rows(r, c):
        total = sq_own[r] + sq_got[0, r] + sq_got[1, r] + sq_got[2, r]
        scale = lax.rsqrt(total[0:1] / (width * TENSOR) + epsilon)
        col = jnp.sum(jnp.where(eye, scale, 0.0), axis=1, keepdims=True)
        for k in range(SPREAD):
            rows = pl.ds(pl.multiple_of(k * 128 + r * QUART, QUART), QUART)
            block = normed[rows, :].astype(F32) * col[k * QUART:(k + 1) * QUART] * gain
            normed[rows, :] = block.astype(BF16)
        return c

    scale_q = 1.0 / math.sqrt(HEAD)
    fresh_no = lax.broadcasted_iota(jnp.int32, (32, 8), 1)
    seen = jnp.logical_and(fresh_no % 2 == 0, fresh_no // 2 <= lax.broadcasted_iota(jnp.int32, (32, 8), 0) // 8)
    cache_no = lax.broadcasted_iota(jnp.int32, (1, 1024), 1)

    def order_queries(layer):
        for head in range(2):
            for step in range(4):
                for g in range(8):
                    begin = (head * 8 + g) * HEAD
                    q_rows[layer * 2 + head, pl.ds(step * 8 + g, 4, stride=32), :] = q_ref[
                        step, layer, :, begin:begin + HEAD].astype(F32)

    def attend_row(layer, head, r):
        q = q_rows[layer * 2 + head, r * 32:(r + 1) * 32, :]
        both = kv_ref[layer, r, :, :, head * HEAD:(head + 1) * HEAD].reshape(1024, HEAD)
        new = fresh_ref[:, layer, r, :, head * HEAD:(head + 1) * HEAD].astype(F32).reshape(8, HEAD)
        valid = jnp.logical_and(cache_no % 2 == 0, cache_no < 2 * meta_ref[0, r:r + 1, 0:1])
        cs = jnp.where(valid, dot_nt(q.astype(BF16), both) * scale_q, masked_score)
        fs = jnp.where(seen, dot_nt(q, new) * scale_q, masked_score)
        peak = jnp.maximum(jnp.max(cs, axis=1, keepdims=True), jnp.max(fs, axis=1, keepdims=True))
        ce = jnp.exp(cs - peak)
        fe = jnp.exp(fs - peak)
        total = jnp.sum(ce, axis=1, keepdims=True) + jnp.sum(fe, axis=1, keepdims=True)
        cw = pltpu.roll(ce / total, 1, 1).astype(BF16)
        fw = (fe / total).astype(BF16).astype(F32)
        res = jnp.dot(cw, both, preferred_element_type=F32)
        res = res + jnp.dot(fw, pltpu.roll(new, 7, 0), preferred_element_type=F32)
        for step in range(4):
            by_row[(step * 4 + r) * 8:(step * 4 + r + 1) * 8, :] = res[step * 8:(step + 1) * 8]

    def attend_end(layer, head):
        for g in range(8):
            begin = layer * width + head * 8 * HEAD + g * HEAD
            heads_ref[:, begin:begin + HEAD] = by_row[pl.ds(g, 16, stride=8), :].astype(BF16)

    order_queries(0)
    order_queries(1)
    gath_w.after_z()
    resp_in.wait()
    lax.fori_loop(0, ROWS_G, turn_rows, 0)
    for d in (1, 2, 3):
        sq_copy(d).start()
    gath_w.after_first(1)
    gath_w.after_first(2)
    kv_in.wait()
    events = {
        1: lambda: gath_w.after_first(3),
        3: lambda: gath_w.after_second(0),
        6: lambda: gath_w.after_second(1),
        9: lambda: gath_w.after_second(2),
        12: lambda: gath_w.after_second(3),
        14: lambda: gath_w.after_onward(0),
    }
    for u in range(16):
        attend_row(u // 8, (u // 4) % 2, u % 4)
        if u % 4 == 3:
            attend_end(u // 8, (u // 4) % 2)
        if u in events:
            events[u]()
    gath_h.start()
    wait_all(sq_got, sqs)
    wait_all(sq_got, sqr)
    lax.fori_loop(0, ROWS_G, norm_rows, 0)
    gath_h.after_z()
    for i in (1, 2, 3):
        gath_w.after_onward(i)
    gath_w.after_across()

    def direction(k):
        return 1 if k >= 2 else -1

    def project(owner, row0, rows):
        zl = lax.div(owner, 2)

        def tile(y_lo, c):
            y = lax.rem(owner, 2) * 2 + y_lo
            wa = gw[0, y, :, zl].reshape(256, half_w)
            wb = gw[1, :, y, zl].reshape(256, half_w)
            res = dot_nt(normed[row0:row0 + rows, :half_w], wa)
            res = res + dot_nt(normed[row0:row0 + rows, half_w:], wb)
            pacc[row0:row0 + rows, pl.ds(pl.multiple_of(y_lo * 256, 256), 256)] = res
            return c

        lax.fori_loop(0, 2, tile, 0)

    def rs_copy(k, step):
        return pltpu.make_async_remote_copy(
            src_ref=rs_send.at[k, step], dst_ref=rs_recv.at[k, step], send_sem=rss.at[0],
            recv_sem=rsr.at[k, step], device_id=(dp, wrap(t + direction(k), 4)), device_id_type=MESH)

    def rot_copy(k):
        rows = scored_ref.at[pl.ds(k * 128, 128), :]
        return pltpu.make_async_remote_copy(
            src_ref=rs_send.at[k, 3], dst_ref=rows, send_sem=rot_s.at[0], recv_sem=rot_r.at[0],
            device_id=(lax.rem(dp + k, groups), t), device_id_type=MESH)

    def project_step(step):
        if step == 1:
            project(wrap(t + 2, 4), 0, 512)
        elif step == 3:
            project(t, 0, 512)
        else:
            project(wrap(t + 1 + step, 4), 0, 256)
            project(wrap(t - 1 - step, 4), 256, 256)

    def pass_step(step, ks):
        for k in ks:
            rows = slice(k * 128, (k + 1) * 128)
            total = pacc[rows, :]
            if step:
                rs_copy(k, step - 1).wait_recv()
                total = total + rs_recv[k, step - 1].astype(F32)
            if step == 3 and k == 0:
                scored_ref[rows, :] = total.astype(BF16)
                continue
            rs_send[k, step] = total.astype(BF16)
            if step < 3:
                rs_copy(k, step).start()
            else:
                rot_copy(k).start()

    project_step(0)
    pass_step(0, (3, 1, 2, 0))
    gath_h.after_first(1)
    gath_h.after_first(2)
    project_step(1)
    gath_h.after_first(3)
    pass_step(1, (3, 1))
    gath_h.after_second(0)
    pass_step(1, (2, 0))
    gath_h.after_second(1)
    project_step(2)
    pass_step(2, (3, 1))
    gath_h.after_second(2)
    pass_step(2, (2, 0))
    gath_h.after_second(3)
    gath_h.after_onward(0)
    project_step(3)
    for i in (1, 2, 3):
        gath_h.after_onward(i)
    gath_h.after_across()

    def decode_part(owner, y_lo):
        zl = lax.div(owner, 2)
        y = lax.rem(owner, 2) * 2 + y_lo
        ha = gh[0, y, :, zl].reshape(128, width)
        hb = gh[1, :, y, zl].reshape(128, width)
        return (jnp.dot(ha, outp_ref[0], preferred_element_type=F32)
                + jnp.dot(hb, outp_ref[1], preferred_element_type=F32))

    def ds_copy(d):
        return pltpu.make_async_remote_copy(
            src_ref=ds_send.at[d - 1], dst_ref=ds_recv.at[3 - d], send_sem=dss.at[0], recv_sem=dsr.at[0],
            device_id=(dp, wrap(t + d, 4)), device_id_type=MESH)

    outp_in.wait()
    for d in (2, 1, 3):
        for y_lo in range(2):
            ds_send[d - 1, y_lo * 128:(y_lo + 1) * 128] = decode_part(wrap(t + d, 4), y_lo).astype(BF16)
        ds_copy(d).start()
    for y_lo in range(2):
        dacc[y_lo] = decode_part(t, y_lo)
    pass_step(3, (3, 1))
    wait_all(ds_recv, dsr)
    for y_lo in range(2):
        total = dacc[y_lo]
        for d in range(3):
            total = total + ds_recv[d, y_lo * 128:(y_lo + 1) * 128].astype(F32)
        dfin[pl.ds(y_lo * 8, 8)] = total.astype(BF16).reshape(8, 16, 128)

    def send_message(i, c):
        d = t * 16 + lax.rem(i, 16)
        dest_t = lax.div(i, 16)
        src = dfin.at[lax.rem(i, 16)]
        dst = dec_ref.at[:, pl.ds(pl.multiple_of(dp * 128, 128), 128)]
        near = jnp.logical_and(d == dp, dest_t == t)

        @pl.when(near)
        def _():
            pltpu.make_async_copy(src, dst, out_r.at[0]).start()

        @pl.when(jnp.logical_not(near))
        def _():
            pltpu.make_async_remote_copy(
                src_ref=src, dst_ref=dst, send_sem=out_s.at[0], recv_sem=out_r.at[0],
                device_id=(d, dest_t), device_id_type=MESH).start()

        return c

    lax.fori_loop(0, 64, send_message, 0)
    pass_step(3, (2, 0))
    wait_all(scored_ref.at[pl.ds(128, 384), :], rot_r)
    wait_all(rs_send.at[pl.ds(1, 3), 3], rot_s)
    wait_all(dec_ref, out_r)

    @pl.when(is_self)
    def _():
        wait_all(dec_ref.at[:, pl.ds(0, 63 * 128)], out_s)

    @pl.when(jnp.logical_not(is_self))
    def _():
        wait_all(dec_ref, out_s)

    wait_all(rs_send.at[:, pl.ds(0, 3)], rss)
    wait_all(ds_send, dss)
    gath_w.end()
    gath_h.end()


def exchange(meta, q, fresh, gain, kv_cache, out_proj, resp_act, wt):
    width = wt.shape[1]
    vmem = pl.BlockSpec(memory_space=pltpu.VMEM)
    dma = pltpu.SemaphoreType.DMA
    return pl.pallas_call(
        kernel,
        out_shape=(
            jax.ShapeDtypeStruct((16, 8192), BF16),
            jax.ShapeDtypeStruct((512, 512), BF16),
        ),
        in_specs=[vmem] * 4 + [pl.BlockSpec(memory_space=pl.ANY)] * 4,
        out_specs=(vmem, vmem),
        scratch_shapes=[
            pltpu.VMEM(kv_cache.shape, BF16),
            pltpu.VMEM(out_proj.shape, BF16),
            pltpu.VMEM(resp_act.shape, BF16),
            pltpu.VMEM((4, 128, 128), F32),
            pltpu.VMEM((16, 2 * width), BF16),
            pltpu.VMEM((128, 128), F32),
            pltpu.VMEM((2, 4, 4, 2, 2, 32, width // 2), BF16),
            pltpu.VMEM((2, 4, 4, 2, 2, 16, width), BF16),
            pltpu.VMEM((512, width), BF16),
            pltpu.VMEM((512, 512), F32),
            pltpu.VMEM((4, 4, 128, 512), BF16),
            pltpu.VMEM((4, 3, 128, 512), BF16),
            pltpu.VMEM((2, 128, 128), F32),
            pltpu.VMEM((3, 256, 128), BF16),
            pltpu.VMEM((3, 256, 128), BF16),
            pltpu.VMEM((16, 16, 128), BF16),
            pltpu.VMEM((4, 8, 128), F32),
            pltpu.VMEM((3, 4, 8, 128), F32),
            dma((6,)), dma((2, 17)), dma((1,)), dma((2,)),
            dma((6,)), dma((2, 17)), dma((1,)), dma((2,)),
            dma((1,)), dma((4, 3)), dma((1,)), dma((1,)),
            dma((1,)), dma((1,)), dma((1,)), dma((1,)), dma((1,)), dma((1,)), dma((3,)),
        ],
        compiler_params=pltpu.CompilerParams(
            collective_id=0, has_side_effects=True, vmem_limit_bytes=56 * 1024 * 1024),
    )(meta, q, fresh, gain, kv_cache, out_proj, resp_act, wt)


def shards(
    queries,
    fresh_kv,
    kv_cache,
    cache_len,
    out_proj,
    finished,
    resp_len,
    start_shard,
    resp_act,
    reward_gain,
    reward_weight,
):
    steps, layers, rows, width = queries.shape
    meta = jnp.stack([cache_len, finished, resp_len, start_shard])
    meta = jnp.broadcast_to(meta[:, :, None], (4, rows, 128))
    dec, scored = exchange(
        meta, queries, fresh_kv, reward_gain.reshape(-1, 128), kv_cache, out_proj, resp_act, reward_weight.T
    )
    return dec.reshape(steps, rows, -1), scored


def solution(mesh):
    return jax.shard_map(
        shards,
        mesh=mesh,
        in_specs=(
            P(None, None, "dp", "tensor"),
            P(None, None, "dp", None, "tensor"),
            P(None, "dp", None, None, "tensor"),
            P("dp"),
            P(None, "tensor", "dp"),
            P("dp"),
            P("dp"),
            P("dp"),
            P("dp", None, "tensor"),
            P("tensor"),
            P("tensor", "dp"),
        ),
        out_specs=(P(None, "dp", None), P("dp", "tensor")),
        check_vma=False,
    )
```

```python
import functools
import math

import jax
import jax.numpy as jnp
from jax import lax
from jax.experimental import pallas as pl
from jax.experimental.pallas import tpu as pltpu
from jax.sharding import PartitionSpec as P

HEAD = 128
SPREAD = 4
QUART = 32
ROWS_G = 4
TENSOR = 4

epsilon = 1e-05
masked_score = -1e30

MESH = pl.DeviceIdType.MESH
STEP_OFF = (0, 1, -1, 2)
BACK = {1: 2, -1: 1}
Z, NEAR, FAR, SECOND, ONWARD, ACROSS = range(6)
F32 = jnp.float32
BF16 = jnp.bfloat16


def wrap(v, n):
    return lax.rem(v + 2 * n, n)


class Place:
    def __init__(self):
        self.dp = lax.axis_index("dp")
        self.t = lax.axis_index("tensor")
        self.core = lax.rem(self.dp, 2)
        self.x = lax.rem(self.dp // 2, 4)
        self.y = lax.rem(self.dp // 8, 4)
        self.zl = self.dp // 32

    def at(self, zl, y, x, core):
        return (((zl * 4 + y) * 4 + x) * 2 + core, self.t)


class Gather:
    def __init__(self, place, own, out, send, recv, cross, local):
        self.p, self.own, self.out, self.send, self.recv = place, own, out, send, recv
        self.cross, self.local = cross, local

    def ring(self, h):
        return (self.p.y, self.p.x) if h == 0 else (self.p.x, self.p.y)

    def dev(self, h, s, f, zl=None, core=None):
        p = self.p
        zl = p.zl if zl is None else zl
        core = p.core if core is None else core
        return p.at(zl, s, f, core) if h == 0 else p.at(zl, f, s, core)

    def unit(self, h, j, core=None):
        s, f = self.ring(h)
        s = wrap(s + STEP_OFF[j // 4], 4)
        f = wrap(f + STEP_OFF[j % 4], 4)
        return self.out.at[h, s, f, :, self.p.core if core is None else core]

    def copy(self, h, src, dst, send, recv, dev):
        return pltpu.make_async_remote_copy(
            src_ref=src, dst_ref=dst, send_sem=self.send.at[send],
            recv_sem=self.cross.at[0] if send == ACROSS else self.recv.at[h, recv],
            device_id=dev, device_id_type=MESH)

    def z_copy(self, h):
        s, f = self.ring(h)
        return self.copy(h, self.own(h), self.out.at[h, s, f, self.p.zl, self.p.core], Z, 0,
                         self.dev(h, s, f, zl=1 - self.p.zl))

    def own_copy(self, h):
        s, f = self.ring(h)
        return pltpu.make_async_copy(self.own(h), self.out.at[h, s, f, self.p.zl, self.p.core], self.local.at[h])

    def start(self):
        for h in range(2):
            s, f = self.ring(h)
            self.z_copy(h).start()
            self.own_copy(h).start()
            self.open_rings(h, self.own(h), self.out.at[h, s, f, self.p.zl, self.p.core])

    def open_rings(self, h, src, dst):
        s, f = self.ring(h)
        for i in (1, 2):
            self.copy(h, src, dst, NEAR, BACK[STEP_OFF[i]], self.dev(h, s, wrap(f + STEP_OFF[i], 4))).start()
        for step, recv in ((1, 8), (-1, 4)):
            self.copy(h, src, dst, SECOND, recv, self.dev(h, wrap(s + step, 4), f)).start()
        self.copy(h, src, dst, ACROSS, 0, self.dev(h, s, f, core=1 - self.p.core)).start()

    def far(self, h, i):
        s, f = self.ring(h)
        u = self.out.at[h, s, wrap(f + STEP_OFF[i], 4), i - 1, self.p.core]
        return self.copy(h, u, u, FAR, 3 if i == 1 else 16, self.dev(h, s, wrap(f - STEP_OFF[i], 4)))

    def second(self, h, i, right):
        s, f = self.ring(h)
        u = self.unit(h, i)
        return self.copy(h, u, u, SECOND, (8 if right else 4) + i, self.dev(h, wrap(s + (1 if right else -1), 4), f))

    def onward(self, h, i):
        s, f = self.ring(h)
        u = self.unit(h, (8 if i < 2 else 4) + i)
        return self.copy(h, u, u, ONWARD, 12 + i, self.dev(h, wrap(s + (1 if i < 2 else -1), 4), f))

    def across(self, h, j):
        s, f = self.ring(h)
        u = self.unit(h, j)
        return self.copy(h, u, u, ACROSS, 0, self.dev(h, s, f, core=1 - self.p.core))

    def wait_for(self, h, ref, recv):
        pltpu.make_async_copy(ref, ref, self.recv.at[h, recv]).wait()

    def arrived(self, h, j):
        self.wait_for(h, self.unit(h, j), j)

    def after_z(self):
        for h in range(2):
            s, f = self.ring(h)
            self.wait_for(h, self.out.at[h, s, f, 1 - self.p.zl, self.p.core], 0)
            u = self.out.at[h, s, f, 1 - self.p.zl, self.p.core]
            self.open_rings(h, u, u)
            self.own_copy(h).wait()

    def after_first(self, i):
        for h in range(2):
            if i < 3:
                self.arrived(h, i)
                self.far(h, i).start()
            else:
                s, f = self.ring(h)
                for zl in range(2):
                    self.wait_for(h, self.out.at[h, s, wrap(f + 2, 4), zl, self.p.core], 16 if zl else 3)
            for right in (True, False):
                self.second(h, i, right).start()
            self.across(h, i).start()

    def after_second(self, i):
        for h in range(2):
            for j in ((8 + i, 4 + i) if i < 2 else (4 + i, 8 + i)):
                self.arrived(h, j)
                if j == (8 if i < 2 else 4) + i:
                    self.onward(h, i).start()
                self.across(h, j).start()

    def after_onward(self, i):
        for h in range(2):
            self.arrived(h, 12 + i)
            self.across(h, 12 + i).start()

    def after_across(self):
        u = self.out.at[:, :, :, :, 1 - self.p.core]
        pltpu.make_async_copy(u, u, self.cross.at[0]).wait()

    def end(self):
        sent = {
            Z: self.out.at[:, 0, 0, 0, 0],
            NEAR: self.out.at[:, 0, pl.ds(0, 2), :, 0],
            FAR: self.out.at[:, 0, 0, :, 0],
            SECOND: self.out.at[:, pl.ds(0, 2), :, :, 0],
            ONWARD: self.out.at[:, 0, :, :, 0],
            ACROSS: self.out.at[:, :, :, :, 0],
        }
        for kind, ref in sent.items():
            pltpu.make_async_copy(ref, ref, self.send.at[kind]).wait()


def eye_mask():
    return lax.broadcasted_iota(jnp.int32, (128, 128), 0) == lax.broadcasted_iota(jnp.int32, (128, 128), 1)


def dot_nt(a, b):
    return lax.dot_general(a, b, (((1,), (1,)), ((), ())), preferred_element_type=F32)


def kernel(
    meta_ref, q_ref, fresh_ref, gain_ref, kv_hbm, outp_hbm, resp_hbm, wt_ref,
    dec_ref, scored_ref,
    kv_ref, outp_ref, resp_ref, q_rows, heads_ref, by_row, gw, gh, normed, pacc, rs_send, rs_recv, dacc, ds_send, ds_recv, dfin, sq_own, sq_got,
    w_send, w_recv, w_cross, w_local, h_send, h_recv, h_cross, h_local,
    rss, rsr, dss, dsr, sqs, sqr, rot_s, rot_r, out_s, out_r, in_s,
):
    p = Place()
    dp, t = p.dp, p.t
    groups = 64
    width = wt_ref.shape[1]
    half_w = width // 2
    is_self = lax.div(dp, 16) == t

    def wait_all(ref, sem):
        pltpu.make_async_copy(ref, ref, sem.at[0]).wait()


    resp_in = pltpu.make_async_copy(resp_hbm, resp_ref, in_s.at[0])
    kv_in = pltpu.make_async_copy(kv_hbm, kv_ref, in_s.at[1])
    outp_in = pltpu.make_async_copy(outp_hbm, outp_ref, in_s.at[2])
    resp_in.start()
    kv_in.start()
    outp_in.start()

    barrier = pltpu.get_barrier_semaphore()

    def greet(dev):
        pl.semaphore_signal(barrier, inc=1, device_id=dev, device_id_type=MESH)

    greet(p.at(1 - p.zl, p.y, p.x, p.core))
    greet(p.at(p.zl, p.y, p.x, 1 - p.core))
    for d in (1, 2, 3):
        greet(p.at(p.zl, p.y, wrap(p.x + d, 4), p.core))
        greet(p.at(p.zl, wrap(p.y + d, 4), p.x, p.core))
        greet((dp, wrap(t + d, 4)))
        greet((wrap(dp - d, groups), t))

    pl.semaphore_wait(barrier, 14)

    gath_w = Gather(p, lambda h: wt_ref.at[:, pl.ds(h * half_w, half_w)], gw, w_send, w_recv, w_cross, w_local)
    gath_h = Gather(p, lambda h: heads_ref.at[:, pl.ds(h * width, width)], gh, h_send, h_recv, h_cross, h_local)
    gath_w.start()

    eye = eye_mask()

    row_no = lax.broadcasted_iota(jnp.int32, (128, 128), 0)
    col_no = lax.broadcasted_iota(jnp.int32, (128, 128), 1)

    def turn_rows(r, c):
        block_no = jnp.bitwise_and(row_no // QUART - meta_ref[3, pl.ds(r, 1), :], SPREAD - 1)
        source = block_no * QUART + jnp.bitwise_and(row_no, QUART - 1)
        live = jnp.logical_and(source < meta_ref[2, pl.ds(r, 1), :], meta_ref[1, pl.ds(r, 1), :] == 1)
        pick = jnp.where(jnp.logical_and(source == col_no, live), 1.0, 0.0).astype(BF16)
        col = jnp.zeros((128, 1), F32)
        for part in range(4):
            cols = slice(part * (width // 4), (part + 1) * (width // 4))
            block = jnp.dot(pick, resp_ref[r, :, cols], preferred_element_type=F32)
            for k in range(SPREAD):
                normed[pl.ds(pl.multiple_of(k * 128 + r * QUART, QUART), QUART), cols] = block[
                    k * QUART:(k + 1) * QUART].astype(BF16)
            col = col + jnp.sum(block * block, axis=1, keepdims=True)
        sq_own[r] = jnp.broadcast_to(jnp.sum(jnp.where(eye, col, 0.0), axis=0, keepdims=True), (8, 128))
        return c

    def sq_copy(d):
        return pltpu.make_async_remote_copy(
            src_ref=sq_own, dst_ref=sq_got.at[3 - d], send_sem=sqs.at[0], recv_sem=sqr.at[0],
            device_id=(dp, wrap(t + d, 4)), device_id_type=MESH)

    gain = jnp.concatenate([gain_ref[i:i + 1, :].astype(F32) for i in range(width // 128)], axis=1)

    def norm_rows(r, c):
        total = sq_own[r] + sq_got[0, r] + sq_got[1, r] + sq_got[2, r]
        scale = lax.rsqrt(total[0:1] / (width * TENSOR) + epsilon)
        col = jnp.sum(jnp.where(eye, scale, 0.0), axis=1, keepdims=True)
        for k in range(SPREAD):
            rows = pl.ds(pl.multiple_of(k * 128 + r * QUART, QUART), QUART)
            block = normed[rows, :].astype(F32) * col[k * QUART:(k + 1) * QUART] * gain
            normed[rows, :] = block.astype(BF16)
        return c

    scale_q = 1.0 / math.sqrt(HEAD)
    fresh_no = lax.broadcasted_iota(jnp.int32, (32, 8), 1)
    seen = jnp.logical_and(fresh_no % 2 == 0, fresh_no // 2 <= lax.broadcasted_iota(jnp.int32, (32, 8), 0) // 8)
    cache_no = lax.broadcasted_iota(jnp.int32, (1, 1024), 1)

    def order_queries(layer):
        for head in range(2):
            for step in range(4):
                for g in range(8):
                    begin = (head * 8 + g) * HEAD
                    q_rows[layer * 2 + head, pl.ds(step * 8 + g, 4, stride=32), :] = q_ref[
                        step, layer, :, begin:begin + HEAD].astype(F32)

    def attend_row(layer, head, r):
        q = q_rows[layer * 2 + head, r * 32:(r + 1) * 32, :]
        both = kv_ref[layer, r, :, :, head * HEAD:(head + 1) * HEAD].reshape(1024, HEAD)
        new = fresh_ref[:, layer, r, :, head * HEAD:(head + 1) * HEAD].astype(F32).reshape(8, HEAD)
        valid = jnp.logical_and(cache_no % 2 == 0, cache_no < 2 * meta_ref[0, r:r + 1, 0:1])
        cs = jnp.where(valid, dot_nt(q.astype(BF16), both) * scale_q, masked_score)
        fs = jnp.where(seen, dot_nt(q, new) * scale_q, masked_score)
        peak = jnp.maximum(jnp.max(cs, axis=1, keepdims=True), jnp.max(fs, axis=1, keepdims=True))
        ce = jnp.exp(cs - peak)
        fe = jnp.exp(fs - peak)
        total = jnp.sum(ce, axis=1, keepdims=True) + jnp.sum(fe, axis=1, keepdims=True)
        cw = pltpu.roll(ce / total, 1, 1).astype(BF16)
        fw = (fe / total).astype(BF16).astype(F32)
        res = jnp.dot(cw, both, preferred_element_type=F32)
        res = res + jnp.dot(fw, pltpu.roll(new, 7, 0), preferred_element_type=F32)
        for step in range(4):
            by_row[(step * 4 + r) * 8:(step * 4 + r + 1) * 8, :] = res[step * 8:(step + 1) * 8]

    def attend_end(layer, head):
        for g in range(8):
            begin = layer * width + head * 8 * HEAD + g * HEAD
            heads_ref[:, begin:begin + HEAD] = by_row[pl.ds(g, 16, stride=8), :].astype(BF16)

    order_queries(0)
    order_queries(1)
    gath_w.after_z()
    resp_in.wait()
    lax.fori_loop(0, ROWS_G, turn_rows, 0)
    for d in (1, 2, 3):
        sq_copy(d).start()
    gath_w.after_first(1)
    gath_w.after_first(2)
    kv_in.wait()
    events = {
        1: lambda: gath_w.after_first(3),
        3: lambda: gath_w.after_second(0),
        6: lambda: gath_w.after_second(1),
        9: lambda: gath_w.after_second(2),
        12: lambda: gath_w.after_second(3),
        14: lambda: gath_w.after_onward(0),
    }
    for u in range(16):
        attend_row(u // 8, (u // 4) % 2, u % 4)
        if u % 4 == 3:
            attend_end(u // 8, (u // 4) % 2)
        if u in events:
            events[u]()
    gath_h.start()
    wait_all(sq_got, sqs)
    wait_all(sq_got, sqr)
    lax.fori_loop(0, ROWS_G, norm_rows, 0)
    gath_h.after_z()
    for i in (1, 2, 3):
        gath_w.after_onward(i)
    gath_w.after_across()

    def direction(k):
        return 1 if k >= 2 else -1

    def project(owner, row0):
        zl = lax.div(owner, 2)
        rows = pl.ds(row0, 256)
        for y_lo in range(2):
            y = lax.rem(owner, 2) * 2 + y_lo
            wa = gw[0, y, :, zl].reshape(256, half_w)
            wb = gw[1, :, y, zl].reshape(256, half_w)
            pacc[rows, y_lo * 256:(y_lo + 1) * 256] = dot_nt(normed[rows, :half_w], wa) + dot_nt(normed[rows, half_w:], wb)

    def rs_copy(k, step):
        return pltpu.make_async_remote_copy(
            src_ref=rs_send.at[k, step], dst_ref=rs_recv.at[k, step], send_sem=rss.at[0],
            recv_sem=rsr.at[k, step], device_id=(dp, wrap(t + direction(k) * (1 if step else -1), 4)), device_id_type=MESH)

    def rot_copy(k):
        return pltpu.make_async_remote_copy(
            src_ref=rs_send.at[k, 3], dst_ref=scored_ref.at[pl.ds(k * 128, 128), :], send_sem=rot_s.at[0],
            recv_sem=rot_r.at[0], device_id=(lax.rem(dp + k, groups), t), device_id_type=MESH)

    def project_step(step):
        def both(i, c):
            project(wrap(t + (1 - 2 * i) * (1 + step), 4), pl.multiple_of(i * 256, 256))
            return c

        lax.fori_loop(0, 2, both, 0)

    def pass_step(step, ks):
        for k in ks:
            total = pacc[k * 128:(k + 1) * 128, :]
            for other in {2: (1,), 3: (0, 2)}.get(step, ()):
                got = rs_recv.at[k, other]
                pltpu.make_async_copy(got, got, rsr.at[k, other]).wait()
                total = total + got[...].astype(F32)
            if step == 3 and k == 0:
                scored_ref[0:128, :] = total.astype(BF16)
                continue
            rs_send[k, step] = total.astype(BF16)
            (rs_copy(k, step) if step < 3 else rot_copy(k)).start()

    def sums(step):
        project_step(step)
        pass_step(step, (3, 1, 2, 0))

    sums(1)
    gath_h.after_first(1)
    gath_h.after_first(2)
    sums(0)
    gath_h.after_first(3)
    gath_h.after_second(0)
    sums(2)
    for i in (1, 2, 3):
        gath_h.after_second(i)
    for i in (0, 1, 2, 3):
        gath_h.after_onward(i)
    gath_h.after_across()

    def decode_part(owner):
        zl = lax.div(owner, 2)
        ys = pl.ds(lax.rem(owner, 2) * 2, 2)
        a = jnp.dot(gh[0, ys, :, zl].reshape(256, width), outp_ref[0], preferred_element_type=F32)
        b = jnp.dot(gh[1, :, ys, zl].reshape(256, width), outp_ref[1], preferred_element_type=F32)
        b = jnp.concatenate([b[x * 64 + y * 32:x * 64 + y * 32 + 32] for y in range(2) for x in range(4)], axis=0)
        return a + b

    def ds_copy(d):
        return pltpu.make_async_remote_copy(
            src_ref=ds_send.at[d - 1], dst_ref=ds_recv.at[3 - d], send_sem=dss.at[0], recv_sem=dsr.at[0],
            device_id=(dp, wrap(t + d, 4)), device_id_type=MESH)

    outp_in.wait()
    for d in (2, 1, 3):
        ds_send[d - 1] = decode_part(wrap(t + d, 4)).astype(BF16)
        ds_copy(d).start()
    dacc[...] = decode_part(t)
    sums(3)
    wait_all(ds_recv, dsr)
    total = dacc[...]
    for d in range(3):
        total = total + ds_recv[d].astype(F32)
    dfin[...] = total.astype(BF16).reshape(16, 16, 128)

    mine = dec_ref.at[:, pl.ds(pl.multiple_of(dp * 128, 128), 128)]

    def message(i, dest_t):
        return pltpu.make_async_remote_copy(
            src_ref=dfin.at[i], dst_ref=mine, send_sem=out_s.at[0], recv_sem=out_r.at[0],
            device_id=(t * 16 + i, dest_t), device_id_type=MESH)

    for off in (2, 1, 3):
        for i in range(16):
            message(i, wrap(t + off, 4)).start()
    for i in range(16):

        @pl.when(t * 16 + i == dp)
        def _():
            pltpu.make_async_copy(dfin.at[i], mine, out_r.at[0]).start()

        @pl.when(t * 16 + i != dp)
        def _():
            message(i, t).start()

    wait_all(scored_ref.at[pl.ds(128, 384), :], rot_r)
    wait_all(rs_send.at[pl.ds(1, 3), 3], rot_s)
    wait_all(dec_ref, out_r)

    @pl.when(is_self)
    def _():
        wait_all(dec_ref.at[:, pl.ds(0, 63 * 128)], out_s)

    @pl.when(jnp.logical_not(is_self))
    def _():
        wait_all(dec_ref, out_s)

    wait_all(rs_send.at[:, pl.ds(0, 3)], rss)
    wait_all(ds_send, dss)
    gath_w.end()
    gath_h.end()


def exchange(meta, q, fresh, gain, kv_cache, out_proj, resp_act, wt):
    width = wt.shape[1]
    vmem = pl.BlockSpec(memory_space=pltpu.VMEM)
    dma = pltpu.SemaphoreType.DMA
    return pl.pallas_call(
        kernel,
        out_shape=(
            jax.ShapeDtypeStruct((16, 8192), BF16),
            jax.ShapeDtypeStruct((512, 512), BF16),
        ),
        in_specs=[vmem] * 4 + [pl.BlockSpec(memory_space=pl.ANY)] * 4,
        out_specs=(vmem, vmem),
        scratch_shapes=[
            pltpu.VMEM(kv_cache.shape, BF16),
            pltpu.VMEM(out_proj.shape, BF16),
            pltpu.VMEM(resp_act.shape, BF16),
            pltpu.VMEM((4, 128, 128), F32),
            pltpu.VMEM((16, 2 * width), BF16),
            pltpu.VMEM((128, 128), F32),
            pltpu.VMEM((2, 4, 4, 2, 2, 32, width // 2), BF16),
            pltpu.VMEM((2, 4, 4, 2, 2, 16, width), BF16),
            pltpu.VMEM((512, width), BF16),
            pltpu.VMEM((512, 512), F32),
            pltpu.VMEM((4, 4, 128, 512), BF16),
            pltpu.VMEM((4, 3, 128, 512), BF16),
            pltpu.VMEM((256, 128), F32),
            pltpu.VMEM((3, 256, 128), BF16),
            pltpu.VMEM((3, 256, 128), BF16),
            pltpu.VMEM((16, 16, 128), BF16),
            pltpu.VMEM((4, 8, 128), F32),
            pltpu.VMEM((3, 4, 8, 128), F32),
            dma((6,)), dma((2, 17)), dma((1,)), dma((2,)),
            dma((6,)), dma((2, 17)), dma((1,)), dma((2,)),
            dma((1,)), dma((4, 3)), dma((1,)), dma((1,)),
            dma((1,)), dma((1,)), dma((1,)), dma((1,)), dma((1,)), dma((1,)), dma((3,)),
        ],
        compiler_params=pltpu.CompilerParams(
            collective_id=0, has_side_effects=True, vmem_limit_bytes=56 * 1024 * 1024),
    )(meta, q, fresh, gain, kv_cache, out_proj, resp_act, wt)


def shards(
    queries,
    fresh_kv,
    kv_cache,
    cache_len,
    out_proj,
    finished,
    resp_len,
    start_shard,
    resp_act,
    reward_gain,
    reward_weight,
):
    steps, layers, rows, width = queries.shape
    meta = jnp.stack([cache_len, finished, resp_len, start_shard])
    meta = jnp.broadcast_to(meta[:, :, None], (4, rows, 128))
    dec, scored = exchange(
        meta, queries, fresh_kv, reward_gain.reshape(-1, 128), kv_cache, out_proj, resp_act, reward_weight.T
    )
    return dec.reshape(steps, rows, -1), scored


def solution(mesh):
    return jax.shard_map(
        shards,
        mesh=mesh,
        in_specs=(
            P(None, None, "dp", "tensor"),
            P(None, None, "dp", None, "tensor"),
            P(None, "dp", None, None, "tensor"),
            P("dp"),
            P(None, "tensor", "dp"),
            P("dp"),
            P("dp"),
            P("dp"),
            P("dp", None, "tensor"),
            P("tensor"),
            P("tensor", "dp"),
        ),
        out_specs=(P(None, "dp", None), P("dp", "tensor")),
        check_vma=False,
    )
```

```python
import functools
import math

import jax
import jax.numpy as jnp
from jax import lax
from jax.experimental import pallas as pl
from jax.experimental.pallas import tpu as pltpu
from jax.sharding import PartitionSpec as P

HEAD = 128
SPREAD = 4
QUART = 32
ROWS_G = 4
TENSOR = 4

epsilon = 1e-05
masked_score = -1e30

MESH = pl.DeviceIdType.MESH
STEP_OFF = (0, 1, -1, 2)
BACK = {1: 2, -1: 1}
Z, NEAR, FAR, SECOND, ONWARD, ACROSS = range(6)
F32 = jnp.float32
BF16 = jnp.bfloat16


def wrap(v, n):
    return lax.rem(v + 2 * n, n)


class Place:
    def __init__(self):
        self.dp = lax.axis_index("dp")
        self.t = lax.axis_index("tensor")
        self.core = lax.rem(self.dp, 2)
        self.x = lax.rem(self.dp // 2, 4)
        self.y = lax.rem(self.dp // 8, 4)
        self.zl = self.dp // 32

    def at(self, zl, y, x, core):
        return (((zl * 4 + y) * 4 + x) * 2 + core, self.t)


class Gather:
    def __init__(self, place, own, out, send, recv, cross, local):
        self.p, self.own, self.out, self.send, self.recv = place, own, out, send, recv
        self.cross, self.local = cross, local

    def ring(self, h):
        return (self.p.y, self.p.x) if h == 0 else (self.p.x, self.p.y)

    def dev(self, h, s, f, zl=None, core=None):
        p = self.p
        zl = p.zl if zl is None else zl
        core = p.core if core is None else core
        return p.at(zl, s, f, core) if h == 0 else p.at(zl, f, s, core)

    def unit(self, h, j, core=None):
        s, f = self.ring(h)
        s = wrap(s + STEP_OFF[j // 4], 4)
        f = wrap(f + STEP_OFF[j % 4], 4)
        return self.out.at[h, s, f, :, self.p.core if core is None else core]

    def copy(self, h, src, dst, send, recv, dev):
        return pltpu.make_async_remote_copy(
            src_ref=src, dst_ref=dst, send_sem=self.send.at[send],
            recv_sem=self.cross.at[0] if send == ACROSS else self.recv.at[h, recv],
            device_id=dev, device_id_type=MESH)

    def z_copy(self, h):
        s, f = self.ring(h)
        return self.copy(h, self.own(h), self.out.at[h, s, f, self.p.zl, self.p.core], Z, 0,
                         self.dev(h, s, f, zl=1 - self.p.zl))

    def own_copy(self, h):
        s, f = self.ring(h)
        return pltpu.make_async_copy(self.own(h), self.out.at[h, s, f, self.p.zl, self.p.core], self.local.at[h])

    def start(self):
        for h in range(2):
            s, f = self.ring(h)
            self.z_copy(h).start()
            self.own_copy(h).start()
            self.open_rings(h, self.own(h), self.out.at[h, s, f, self.p.zl, self.p.core])

    def open_rings(self, h, src, dst):
        s, f = self.ring(h)
        for i in (1, 2):
            self.copy(h, src, dst, NEAR, BACK[STEP_OFF[i]], self.dev(h, s, wrap(f + STEP_OFF[i], 4))).start()
        for step, recv in ((1, 8), (-1, 4)):
            self.copy(h, src, dst, SECOND, recv, self.dev(h, wrap(s + step, 4), f)).start()
        self.copy(h, src, dst, ACROSS, 0, self.dev(h, s, f, core=1 - self.p.core)).start()

    def far(self, h, i):
        s, f = self.ring(h)
        u = self.out.at[h, s, wrap(f + STEP_OFF[i], 4), i - 1, self.p.core]
        return self.copy(h, u, u, FAR, 3 if i == 1 else 16, self.dev(h, s, wrap(f - STEP_OFF[i], 4)))

    def second(self, h, i, right):
        s, f = self.ring(h)
        u = self.unit(h, i)
        return self.copy(h, u, u, SECOND, (8 if right else 4) + i, self.dev(h, wrap(s + (1 if right else -1), 4), f))

    def onward(self, h, i):
        s, f = self.ring(h)
        u = self.unit(h, (8 if i < 2 else 4) + i)
        return self.copy(h, u, u, ONWARD, 12 + i, self.dev(h, wrap(s + (1 if i < 2 else -1), 4), f))

    def across(self, h, j):
        s, f = self.ring(h)
        u = self.unit(h, j)
        return self.copy(h, u, u, ACROSS, 0, self.dev(h, s, f, core=1 - self.p.core))

    def wait_for(self, h, ref, recv):
        pltpu.make_async_copy(ref, ref, self.recv.at[h, recv]).wait()

    def arrived(self, h, j):
        self.wait_for(h, self.unit(h, j), j)

    def after_z(self):
        for h in range(2):
            s, f = self.ring(h)
            self.wait_for(h, self.out.at[h, s, f, 1 - self.p.zl, self.p.core], 0)
            u = self.out.at[h, s, f, 1 - self.p.zl, self.p.core]
            self.open_rings(h, u, u)
            self.own_copy(h).wait()

    def after_first(self, i):
        for h in range(2):
            if i < 3:
                self.arrived(h, i)
                self.far(h, i).start()
            else:
                s, f = self.ring(h)
                for zl in range(2):
                    self.wait_for(h, self.out.at[h, s, wrap(f + 2, 4), zl, self.p.core], 16 if zl else 3)
            for right in (True, False):
                self.second(h, i, right).start()
            self.across(h, i).start()

    def after_second(self, i):
        for h in range(2):
            for j in ((8 + i, 4 + i) if i < 2 else (4 + i, 8 + i)):
                self.arrived(h, j)
                if j == (8 if i < 2 else 4) + i:
                    self.onward(h, i).start()
                self.across(h, j).start()

    def after_onward(self, i):
        for h in range(2):
            self.arrived(h, 12 + i)
            self.across(h, 12 + i).start()

    def after_across(self):
        u = self.out.at[:, :, :, :, 1 - self.p.core]
        pltpu.make_async_copy(u, u, self.cross.at[0]).wait()

    def end(self):
        sent = {
            Z: self.out.at[:, 0, 0, 0, 0],
            NEAR: self.out.at[:, 0, pl.ds(0, 2), :, 0],
            FAR: self.out.at[:, 0, 0, :, 0],
            SECOND: self.out.at[:, pl.ds(0, 2), :, :, 0],
            ONWARD: self.out.at[:, 0, :, :, 0],
            ACROSS: self.out.at[:, :, :, :, 0],
        }
        for kind, ref in sent.items():
            pltpu.make_async_copy(ref, ref, self.send.at[kind]).wait()


def eye_mask():
    return lax.broadcasted_iota(jnp.int32, (128, 128), 0) == lax.broadcasted_iota(jnp.int32, (128, 128), 1)


def dot_nt(a, b):
    return lax.dot_general(a, b, (((1,), (1,)), ((), ())), preferred_element_type=F32)


def kernel(
    meta_ref, q_ref, fresh_ref, gain_ref, kv_hbm, outp_hbm, resp_hbm, wt_ref,
    dec_ref, scored_ref,
    kv_ref, outp_ref, resp_ref, q_rows, heads_ref, by_row, gw_a, gw_b, gh, normed, pacc, rs_send, rs_recv, first_part, whole, place_cols, dacc, ds_send, ds_recv, dfin, sq_own, sq_got,
    wa_send, wa_recv, wa_cross, wa_local, wb_send, wb_recv, wb_cross, wb_local, h_send, h_recv, h_cross, h_local,
    rss, rsr, dss, dsr, sqs, sqr, rot_s, rot_r, out_s, out_r, in_s,
):
    p = Place()
    dp, t = p.dp, p.t
    groups = 64
    width = wt_ref.shape[1]
    half_w = width // 2
    is_self = lax.div(dp, 16) == t

    def wait_all(ref, sem):
        pltpu.make_async_copy(ref, ref, sem.at[0]).wait()


    resp_in = pltpu.make_async_copy(resp_hbm, resp_ref, in_s.at[0])
    kv_in = pltpu.make_async_copy(kv_hbm, kv_ref, in_s.at[1])
    outp_in = pltpu.make_async_copy(outp_hbm, outp_ref, in_s.at[2])
    resp_in.start()
    kv_in.start()
    outp_in.start()

    barrier = pltpu.get_barrier_semaphore()

    def greet(dev):
        pl.semaphore_signal(barrier, inc=1, device_id=dev, device_id_type=MESH)

    greet(p.at(1 - p.zl, p.y, p.x, p.core))
    greet(p.at(p.zl, p.y, p.x, 1 - p.core))
    for d in (1, 2, 3):
        greet(p.at(p.zl, p.y, wrap(p.x + d, 4), p.core))
        greet(p.at(p.zl, wrap(p.y + d, 4), p.x, p.core))
        greet((dp, wrap(t + d, 4)))
        greet((wrap(dp - d, groups), t))

    pl.semaphore_wait(barrier, 14)

    gw = (gw_a, gw_b)
    gath_a = Gather(p, lambda h: wt_ref.at[pl.ds(0, 16), pl.ds(h * half_w, half_w)], gw_a, wa_send, wa_recv, wa_cross, wa_local)
    gath_b = Gather(p, lambda h: wt_ref.at[pl.ds(16, 16), pl.ds(h * half_w, half_w)], gw_b, wb_send, wb_recv, wb_cross, wb_local)
    gath_h = Gather(p, lambda h: heads_ref.at[:, pl.ds(h * width, width)], gh, h_send, h_recv, h_cross, h_local)
    gath_a.start()
    gath_b.start()

    eye = eye_mask()

    row_no = lax.broadcasted_iota(jnp.int32, (128, 128), 0)
    col_no = lax.broadcasted_iota(jnp.int32, (128, 128), 1)

    def turn_rows(r, c):
        block_no = jnp.bitwise_and(row_no // QUART - meta_ref[3, pl.ds(r, 1), :], SPREAD - 1)
        source = block_no * QUART + jnp.bitwise_and(row_no, QUART - 1)
        live = jnp.logical_and(source < meta_ref[2, pl.ds(r, 1), :], meta_ref[1, pl.ds(r, 1), :] == 1)
        pick = jnp.where(jnp.logical_and(source == col_no, live), 1.0, 0.0).astype(BF16)
        col = jnp.zeros((128, 1), F32)
        for part in range(4):
            cols = slice(part * (width // 4), (part + 1) * (width // 4))
            block = jnp.dot(pick, resp_ref[r, :, cols], preferred_element_type=F32)
            for k in range(SPREAD):
                normed[pl.ds(pl.multiple_of(k * 128 + r * QUART, QUART), QUART), cols] = block[
                    k * QUART:(k + 1) * QUART].astype(BF16)
            col = col + jnp.sum(block * block, axis=1, keepdims=True)
        sq_own[r] = jnp.broadcast_to(jnp.sum(jnp.where(eye, col, 0.0), axis=0, keepdims=True), (8, 128))
        return c

    def sq_copy(d):
        return pltpu.make_async_remote_copy(
            src_ref=sq_own, dst_ref=sq_got.at[3 - d], send_sem=sqs.at[0], recv_sem=sqr.at[0],
            device_id=(dp, wrap(t + d, 4)), device_id_type=MESH)

    gain = jnp.concatenate([gain_ref[i:i + 1, :].astype(F32) for i in range(width // 128)], axis=1)

    def norm_rows(r, c):
        total = sq_own[r] + sq_got[0, r] + sq_got[1, r] + sq_got[2, r]
        scale = lax.rsqrt(total[0:1] / (width * TENSOR) + epsilon)
        col = jnp.sum(jnp.where(eye, scale, 0.0), axis=1, keepdims=True)
        for k in range(SPREAD):
            rows = pl.ds(pl.multiple_of(k * 128 + r * QUART, QUART), QUART)
            block = normed[rows, :].astype(F32) * col[k * QUART:(k + 1) * QUART] * gain
            normed[rows, :] = block.astype(BF16)
        return c

    scale_q = 1.0 / math.sqrt(HEAD)
    fresh_no = lax.broadcasted_iota(jnp.int32, (32, 8), 1)
    seen = jnp.logical_and(fresh_no % 2 == 0, fresh_no // 2 <= lax.broadcasted_iota(jnp.int32, (32, 8), 0) // 8)
    cache_no = lax.broadcasted_iota(jnp.int32, (1, 1024), 1)

    def order_queries(layer):
        for head in range(2):
            for step in range(4):
                for g in range(8):
                    begin = (head * 8 + g) * HEAD
                    q_rows[layer * 2 + head, pl.ds(step * 8 + g, 4, stride=32), :] = q_ref[
                        step, layer, :, begin:begin + HEAD].astype(F32)

    def attend_row(layer, head, r):
        q = q_rows[layer * 2 + head, r * 32:(r + 1) * 32, :]
        both = kv_ref[layer, r, :, :, head * HEAD:(head + 1) * HEAD].reshape(1024, HEAD)
        new = fresh_ref[:, layer, r, :, head * HEAD:(head + 1) * HEAD].astype(F32).reshape(8, HEAD)
        valid = jnp.logical_and(cache_no % 2 == 0, cache_no < 2 * meta_ref[0, r:r + 1, 0:1])
        cs = jnp.where(valid, dot_nt(q.astype(BF16), both) * scale_q, masked_score)
        fs = jnp.where(seen, dot_nt(q, new) * scale_q, masked_score)
        peak = jnp.maximum(jnp.max(cs, axis=1, keepdims=True), jnp.max(fs, axis=1, keepdims=True))
        ce = jnp.exp(cs - peak)
        fe = jnp.exp(fs - peak)
        total = jnp.sum(ce, axis=1, keepdims=True) + jnp.sum(fe, axis=1, keepdims=True)
        cw = pltpu.roll(ce / total, 1, 1).astype(BF16)
        fw = (fe / total).astype(BF16).astype(F32)
        res = jnp.dot(cw, both, preferred_element_type=F32)
        res = res + jnp.dot(fw, pltpu.roll(new, 7, 0), preferred_element_type=F32)
        for step in range(4):
            by_row[(step * 4 + r) * 8:(step * 4 + r + 1) * 8, :] = res[step * 8:(step + 1) * 8]

    def attend_end(layer, head):
        for g in range(8):
            begin = layer * width + head * 8 * HEAD + g * HEAD
            heads_ref[:, begin:begin + HEAD] = by_row[pl.ds(g, 16, stride=8), :].astype(BF16)

    def units(begin, end):
        for u in range(begin, end):
            attend_row(u // 8, (u // 4) % 2, u % 4)
            if u % 4 == 3:
                attend_end(u // 8, (u // 4) % 2)

    def direction(k):
        return 1 if k >= 2 else -1

    def project(part, owner, row0):
        zl = lax.div(owner, 2)
        ys = [lax.rem(owner, 2) * 2 + y_lo for y_lo in range(2)]
        wa = jnp.concatenate([gw[part][0, y, :, zl].reshape(128, half_w) for y in ys], axis=0)
        wb = jnp.concatenate([gw[part][1, :, y, zl].reshape(128, half_w) for y in ys], axis=0)
        rows = pl.ds(row0, 256)
        pacc[rows, :] = dot_nt(normed[rows, :half_w], wa) + dot_nt(normed[rows, half_w:], wb)

    def rs_copy(part, k, step):
        return pltpu.make_async_remote_copy(
            src_ref=rs_send.at[part, k, step], dst_ref=rs_recv.at[part, k, step], send_sem=rss.at[0],
            recv_sem=rsr.at[part, k, step], device_id=(dp, wrap(t + direction(k) * (1 if step else -1), 4)), device_id_type=MESH)

    def rot_copy(k):
        return pltpu.make_async_remote_copy(
            src_ref=whole.at[k - 1], dst_ref=scored_ref.at[pl.ds(k * 128, 128), :], send_sem=rot_s.at[0],
            recv_sem=rot_r.at[0], device_id=(lax.rem(dp + k, groups), t), device_id_type=MESH)

    def project_step(part, step):
        def both(i, c):
            project(part, wrap(t + (1 - 2 * i) * (1 + step), 4), pl.multiple_of(i * 256, 256))
            return c

        lax.fori_loop(0, 2, both, 0)

    def pass_step(part, step, ks):
        for k in ks:
            total = pacc[k * 128:(k + 1) * 128, :]
            for other in {2: (1,), 3: (0, 2)}.get(step, ()):
                got = rs_recv.at[part, k, other]
                pltpu.make_async_copy(got, got, rsr.at[part, k, other]).wait()
                total = total + got[...].astype(F32)
            total = total.astype(BF16)
            if step < 3:
                rs_send[part, k, step] = total
                rs_copy(part, k, step).start()
            elif part == 0:
                first_part[k] = total
            else:
                rows = jnp.dot(first_part[k], place_cols[0], preferred_element_type=F32)
                rows = (rows + jnp.dot(total, place_cols[1], preferred_element_type=F32)).astype(BF16)
                if k == 0:
                    scored_ref[0:128, :] = rows
                else:
                    whole[k - 1] = rows
                    rot_copy(k).start()

    line_no = lax.broadcasted_iota(jnp.int32, (256, 512), 0)
    goal_no = lax.broadcasted_iota(jnp.int32, (256, 512), 1)
    for part in range(2):
        goal = line_no // 16 * 32 + part * 16 + jnp.bitwise_and(line_no, 15)
        place_cols[part] = jnp.where(goal == goal_no, 1.0, 0.0).astype(BF16)

    def sums(part, step):
        project_step(part, step)
        pass_step(part, step, (3, 1, 2, 0))

    order_queries(0)
    order_queries(1)
    gath_a.after_z()
    resp_in.wait()
    lax.fori_loop(0, ROWS_G, turn_rows, 0)
    for d in (1, 2, 3):
        sq_copy(d).start()
    gath_a.after_first(1)
    gath_a.after_first(2)
    kv_in.wait()
    units(0, 2)
    gath_a.after_first(3)
    units(2, 3)
    gath_a.after_second(0)
    gath_a.after_second(1)
    units(3, 4)
    gath_b.after_z()
    gath_a.after_second(2)
    gath_a.after_second(3)
    wait_all(sq_got, sqs)
    wait_all(sq_got, sqr)
    lax.fori_loop(0, ROWS_G, norm_rows, 0)
    gath_b.after_first(1)
    gath_b.after_first(2)
    for i in range(4):
        gath_a.after_onward(i)
    gath_b.after_first(3)
    gath_a.after_across()
    sums(0, 1)
    sums(0, 0)
    gath_b.after_second(0)
    units(4, 7)
    gath_b.after_second(1)
    units(7, 10)
    gath_b.after_second(2)
    units(10, 13)
    gath_b.after_second(3)
    units(13, 16)
    gath_h.start()
    for i in range(4):
        gath_b.after_onward(i)
    gath_h.after_z()
    sums(0, 2)
    gath_b.after_across()
    sums(1, 1)
    gath_h.after_first(1)
    gath_h.after_first(2)
    sums(1, 0)
    gath_h.after_first(3)
    gath_h.after_second(0)
    sums(0, 3)
    gath_h.after_second(1)
    sums(1, 2)
    for i in (2, 3):
        gath_h.after_second(i)
    for i in (0, 1, 2, 3):
        gath_h.after_onward(i)
    gath_h.after_across()

    def decode_part(owner):
        zl = lax.div(owner, 2)
        ys = pl.ds(lax.rem(owner, 2) * 2, 2)
        a = jnp.dot(gh[0, ys, :, zl].reshape(256, width), outp_ref[0], preferred_element_type=F32)
        b = jnp.dot(gh[1, :, ys, zl].reshape(256, width), outp_ref[1], preferred_element_type=F32)
        b = jnp.concatenate([b[x * 64 + y * 32:x * 64 + y * 32 + 32] for y in range(2) for x in range(4)], axis=0)
        return a + b

    def ds_copy(d):
        return pltpu.make_async_remote_copy(
            src_ref=ds_send.at[d - 1], dst_ref=ds_recv.at[3 - d], send_sem=dss.at[0], recv_sem=dsr.at[0],
            device_id=(dp, wrap(t + d, 4)), device_id_type=MESH)

    outp_in.wait()
    for d in (2, 1, 3):
        ds_send[d - 1] = decode_part(wrap(t + d, 4)).astype(BF16)
        ds_copy(d).start()
    dacc[...] = decode_part(t)
    sums(1, 3)
    wait_all(ds_recv, dsr)
    total = dacc[...]
    for d in range(3):
        total = total + ds_recv[d].astype(F32)
    dfin[...] = total.astype(BF16).reshape(16, 16, 128)

    mine = dec_ref.at[:, pl.ds(pl.multiple_of(dp * 128, 128), 128)]

    def message(i, dest_t):
        return pltpu.make_async_remote_copy(
            src_ref=dfin.at[i], dst_ref=mine, send_sem=out_s.at[0], recv_sem=out_r.at[0],
            device_id=(t * 16 + i, dest_t), device_id_type=MESH)

    for off in (2, 1, 3):
        for i in range(16):
            message(i, wrap(t + off, 4)).start()
    for i in range(16):

        @pl.when(t * 16 + i == dp)
        def _():
            pltpu.make_async_copy(dfin.at[i], mine, out_r.at[0]).start()

        @pl.when(t * 16 + i != dp)
        def _():
            message(i, t).start()

    wait_all(scored_ref.at[pl.ds(128, 384), :], rot_r)
    wait_all(whole, rot_s)
    wait_all(dec_ref, out_r)

    @pl.when(is_self)
    def _():
        wait_all(dec_ref.at[:, pl.ds(0, 63 * 128)], out_s)

    @pl.when(jnp.logical_not(is_self))
    def _():
        wait_all(dec_ref, out_s)

    wait_all(rs_send, rss)
    wait_all(ds_send, dss)
    gath_a.end()
    gath_b.end()
    gath_h.end()


def exchange(meta, q, fresh, gain, kv_cache, out_proj, resp_act, wt):
    width = wt.shape[1]
    vmem = pl.BlockSpec(memory_space=pltpu.VMEM)
    dma = pltpu.SemaphoreType.DMA
    return pl.pallas_call(
        kernel,
        out_shape=(
            jax.ShapeDtypeStruct((16, 8192), BF16),
            jax.ShapeDtypeStruct((512, 512), BF16),
        ),
        in_specs=[vmem] * 4 + [pl.BlockSpec(memory_space=pl.ANY)] * 4,
        out_specs=(vmem, vmem),
        scratch_shapes=[
            pltpu.VMEM(kv_cache.shape, BF16),
            pltpu.VMEM(out_proj.shape, BF16),
            pltpu.VMEM(resp_act.shape, BF16),
            pltpu.VMEM((4, 128, 128), F32),
            pltpu.VMEM((16, 2 * width), BF16),
            pltpu.VMEM((128, 128), F32),
            pltpu.VMEM((2, 4, 4, 2, 2, 16, width // 2), BF16),
            pltpu.VMEM((2, 4, 4, 2, 2, 16, width // 2), BF16),
            pltpu.VMEM((2, 4, 4, 2, 2, 16, width), BF16),
            pltpu.VMEM((512, width), BF16),
            pltpu.VMEM((512, 256), F32),
            pltpu.VMEM((2, 4, 3, 128, 256), BF16),
            pltpu.VMEM((2, 4, 3, 128, 256), BF16),
            pltpu.VMEM((4, 128, 256), BF16),
            pltpu.VMEM((3, 128, 512), BF16),
            pltpu.VMEM((2, 256, 512), BF16),
            pltpu.VMEM((256, 128), F32),
            pltpu.VMEM((3, 256, 128), BF16),
            pltpu.VMEM((3, 256, 128), BF16),
            pltpu.VMEM((16, 16, 128), BF16),
            pltpu.VMEM((4, 8, 128), F32),
            pltpu.VMEM((3, 4, 8, 128), F32),
            dma((6,)), dma((2, 17)), dma((1,)), dma((2,)),
            dma((6,)), dma((2, 17)), dma((1,)), dma((2,)),
            dma((6,)), dma((2, 17)), dma((1,)), dma((2,)),
            dma((1,)), dma((2, 4, 3)), dma((1,)), dma((1,)),
            dma((1,)), dma((1,)), dma((1,)), dma((1,)), dma((1,)), dma((1,)), dma((3,)),
        ],
        compiler_params=pltpu.CompilerParams(
            collective_id=0, has_side_effects=True, vmem_limit_bytes=56 * 1024 * 1024),
    )(meta, q, fresh, gain, kv_cache, out_proj, resp_act, wt)


def shards(
    queries,
    fresh_kv,
    kv_cache,
    cache_len,
    out_proj,
    finished,
    resp_len,
    start_shard,
    resp_act,
    reward_gain,
    reward_weight,
):
    steps, layers, rows, width = queries.shape
    meta = jnp.stack([cache_len, finished, resp_len, start_shard])
    meta = jnp.broadcast_to(meta[:, :, None], (4, rows, 128))
    dec, scored = exchange(
        meta, queries, fresh_kv, reward_gain.reshape(-1, 128), kv_cache, out_proj, resp_act, reward_weight.T
    )
    return dec.reshape(steps, rows, -1), scored


def solution(mesh):
    return jax.shard_map(
        shards,
        mesh=mesh,
        in_specs=(
            P(None, None, "dp", "tensor"),
            P(None, None, "dp", None, "tensor"),
            P(None, "dp", None, None, "tensor"),
            P("dp"),
            P(None, "tensor", "dp"),
            P("dp"),
            P("dp"),
            P("dp"),
            P("dp", None, "tensor"),
            P("tensor"),
            P("tensor", "dp"),
        ),
        out_specs=(P(None, "dp", None), P("dp", "tensor")),
        check_vma=False,
    )
```

```python
import functools
import math

import jax
import jax.numpy as jnp
from jax import lax
from jax.experimental import pallas as pl
from jax.experimental.pallas import tpu as pltpu
from jax.sharding import PartitionSpec as P

HEAD = 128
SPREAD = 4
QUART = 32
ROWS_G = 4
TENSOR = 4

epsilon = 1e-05
masked_score = -1e30

MESH = pl.DeviceIdType.MESH
STEP_OFF = (0, 1, -1, 2)
BACK = {1: 2, -1: 1}
Z, NEAR, FAR, SECOND, ONWARD, ACROSS = range(6)
F32 = jnp.float32
BF16 = jnp.bfloat16


def wrap(v, n):
    return lax.rem(v + 2 * n, n)


class Place:
    def __init__(self):
        self.dp = lax.axis_index("dp")
        self.t = lax.axis_index("tensor")
        self.core = lax.rem(self.dp, 2)
        self.x = lax.rem(self.dp // 2, 4)
        self.y = lax.rem(self.dp // 8, 4)
        self.zl = self.dp // 32

    def at(self, zl, y, x, core):
        return (((zl * 4 + y) * 4 + x) * 2 + core, self.t)


class Gather:
    def __init__(self, place, own, out, send, recv, cross, local):
        self.p, self.own, self.out, self.send, self.recv = place, own, out, send, recv
        self.cross, self.local = cross, local

    def ring(self, h):
        return (self.p.y, self.p.x) if h == 0 else (self.p.x, self.p.y)

    def dev(self, h, s, f, zl=None, core=None):
        p = self.p
        zl = p.zl if zl is None else zl
        core = p.core if core is None else core
        return p.at(zl, s, f, core) if h == 0 else p.at(zl, f, s, core)

    def unit(self, h, j, core=None):
        s, f = self.ring(h)
        s = wrap(s + STEP_OFF[j // 4], 4)
        f = wrap(f + STEP_OFF[j % 4], 4)
        return self.out.at[h, s, f, :, self.p.core if core is None else core]

    def copy(self, h, src, dst, send, recv, dev):
        return pltpu.make_async_remote_copy(
            src_ref=src, dst_ref=dst, send_sem=self.send.at[send],
            recv_sem=self.cross.at[0] if send == ACROSS else self.recv.at[h, recv],
            device_id=dev, device_id_type=MESH)

    def z_copy(self, h):
        s, f = self.ring(h)
        return self.copy(h, self.own(h), self.out.at[h, s, f, self.p.zl, self.p.core], Z, 0,
                         self.dev(h, s, f, zl=1 - self.p.zl))

    def own_copy(self, h):
        s, f = self.ring(h)
        return pltpu.make_async_copy(self.own(h), self.out.at[h, s, f, self.p.zl, self.p.core], self.local.at[h])

    def start(self):
        for h in range(2):
            s, f = self.ring(h)
            self.z_copy(h).start()
            self.own_copy(h).start()
            self.open_rings(h, self.own(h), self.out.at[h, s, f, self.p.zl, self.p.core])

    def open_rings(self, h, src, dst):
        s, f = self.ring(h)
        for i in (1, 2):
            self.copy(h, src, dst, NEAR, BACK[STEP_OFF[i]], self.dev(h, s, wrap(f + STEP_OFF[i], 4))).start()
        for step, recv in ((1, 8), (-1, 4)):
            self.copy(h, src, dst, SECOND, recv, self.dev(h, wrap(s + step, 4), f)).start()
        self.copy(h, src, dst, ACROSS, 0, self.dev(h, s, f, core=1 - self.p.core)).start()

    def far(self, h, i):
        s, f = self.ring(h)
        u = self.out.at[h, s, wrap(f + STEP_OFF[i], 4), i - 1, self.p.core]
        return self.copy(h, u, u, FAR, 3 if i == 1 else 16, self.dev(h, s, wrap(f - STEP_OFF[i], 4)))

    def second(self, h, i, right):
        s, f = self.ring(h)
        u = self.unit(h, i)
        return self.copy(h, u, u, SECOND, (8 if right else 4) + i, self.dev(h, wrap(s + (1 if right else -1), 4), f))

    def onward(self, h, i):
        s, f = self.ring(h)
        u = self.unit(h, (8 if i < 2 else 4) + i)
        return self.copy(h, u, u, ONWARD, 12 + i, self.dev(h, wrap(s + (1 if i < 2 else -1), 4), f))

    def across(self, h, j):
        s, f = self.ring(h)
        u = self.unit(h, j)
        return self.copy(h, u, u, ACROSS, 0, self.dev(h, s, f, core=1 - self.p.core))

    def wait_for(self, h, ref, recv):
        pltpu.make_async_copy(ref, ref, self.recv.at[h, recv]).wait()

    def arrived(self, h, j):
        self.wait_for(h, self.unit(h, j), j)

    def after_z(self):
        for h in range(2):
            s, f = self.ring(h)
            self.wait_for(h, self.out.at[h, s, f, 1 - self.p.zl, self.p.core], 0)
            u = self.out.at[h, s, f, 1 - self.p.zl, self.p.core]
            self.open_rings(h, u, u)
            self.own_copy(h).wait()

    def after_first(self, i):
        for h in range(2):
            if i < 3:
                self.arrived(h, i)
                self.far(h, i).start()
            else:
                s, f = self.ring(h)
                for zl in range(2):
                    self.wait_for(h, self.out.at[h, s, wrap(f + 2, 4), zl, self.p.core], 16 if zl else 3)
            for right in (True, False):
                self.second(h, i, right).start()
            self.across(h, i).start()

    def after_second(self, i):
        for h in range(2):
            for j in ((8 + i, 4 + i) if i < 2 else (4 + i, 8 + i)):
                self.arrived(h, j)
                if j == (8 if i < 2 else 4) + i:
                    self.onward(h, i).start()
                self.across(h, j).start()

    def after_onward(self, i):
        for h in range(2):
            self.arrived(h, 12 + i)
            self.across(h, 12 + i).start()

    def after_across(self):
        u = self.out.at[:, :, :, :, 1 - self.p.core]
        pltpu.make_async_copy(u, u, self.cross.at[0]).wait()

    def end(self):
        sent = {
            Z: self.out.at[:, 0, 0, 0, 0],
            NEAR: self.out.at[:, 0, pl.ds(0, 2), :, 0],
            FAR: self.out.at[:, 0, 0, :, 0],
            SECOND: self.out.at[:, pl.ds(0, 2), :, :, 0],
            ONWARD: self.out.at[:, 0, :, :, 0],
            ACROSS: self.out.at[:, :, :, :, 0],
        }
        for kind, ref in sent.items():
            pltpu.make_async_copy(ref, ref, self.send.at[kind]).wait()


def eye_mask():
    return lax.broadcasted_iota(jnp.int32, (128, 128), 0) == lax.broadcasted_iota(jnp.int32, (128, 128), 1)


def dot_nt(a, b):
    return lax.dot_general(a, b, (((1,), (1,)), ((), ())), preferred_element_type=F32)


def kernel(
    meta_ref, q_ref, fresh_ref, gain_ref, kv_hbm, outp_hbm, resp_hbm, wt_ref,
    dec_ref, scored_ref,
    kv_ref, outp_ref, resp_ref, q_rows, heads_ref, by_row, gw_a, gw_b, gh, normed, pacc, rs_send, rs_recv, first_part, whole, place_cols, dacc, ds_send, ds_recv, dfin, sq_own, sq_got,
    wa_send, wa_recv, wa_cross, wa_local, wb_send, wb_recv, wb_cross, wb_local, h_send, h_recv, h_cross, h_local,
    rss, rsr, dss, dsr, sqs, sqr, rot_s, rot_r, out_s, out_r, in_s,
):
    p = Place()
    dp, t = p.dp, p.t
    groups = 64
    width = wt_ref.shape[1]
    half_w = width // 2
    is_self = lax.div(dp, 16) == t

    def wait_all(ref, sem):
        pltpu.make_async_copy(ref, ref, sem.at[0]).wait()


    resp_in = pltpu.make_async_copy(resp_hbm, resp_ref, in_s.at[0])
    kv_in = pltpu.make_async_copy(kv_hbm, kv_ref, in_s.at[1])
    outp_in = pltpu.make_async_copy(outp_hbm, outp_ref, in_s.at[2])
    resp_in.start()
    kv_in.start()
    outp_in.start()

    barrier = pltpu.get_barrier_semaphore()

    def greet(dev):
        pl.semaphore_signal(barrier, inc=1, device_id=dev, device_id_type=MESH)

    greet(p.at(1 - p.zl, p.y, p.x, p.core))
    greet(p.at(p.zl, p.y, p.x, 1 - p.core))
    for d in (1, 2, 3):
        greet(p.at(p.zl, p.y, wrap(p.x + d, 4), p.core))
        greet(p.at(p.zl, wrap(p.y + d, 4), p.x, p.core))
        greet((dp, wrap(t + d, 4)))
        greet((wrap(dp - d, groups), t))

    pl.semaphore_wait(barrier, 14)

    gw = (gw_a, gw_b)
    gath_a = Gather(p, lambda h: wt_ref.at[pl.ds(0, 16), pl.ds(h * half_w, half_w)], gw_a, wa_send, wa_recv, wa_cross, wa_local)
    gath_b = Gather(p, lambda h: wt_ref.at[pl.ds(16, 16), pl.ds(h * half_w, half_w)], gw_b, wb_send, wb_recv, wb_cross, wb_local)
    gath_h = Gather(p, lambda h: heads_ref.at[:, pl.ds(h * width, width)], gh, h_send, h_recv, h_cross, h_local)
    gath_a.start()
    gath_b.start()

    eye = eye_mask()

    row_no = lax.broadcasted_iota(jnp.int32, (128, 128), 0)
    col_no = lax.broadcasted_iota(jnp.int32, (128, 128), 1)

    def turn_rows(r, c):
        block_no = jnp.bitwise_and(row_no // QUART - meta_ref[3, pl.ds(r, 1), :], SPREAD - 1)
        source = block_no * QUART + jnp.bitwise_and(row_no, QUART - 1)
        live = jnp.logical_and(source < meta_ref[2, pl.ds(r, 1), :], meta_ref[1, pl.ds(r, 1), :] == 1)
        pick = jnp.where(jnp.logical_and(source == col_no, live), 1.0, 0.0).astype(BF16)
        col = jnp.zeros((128, 1), F32)
        for part in range(4):
            cols = slice(part * (width // 4), (part + 1) * (width // 4))
            block = jnp.dot(pick, resp_ref[r, :, cols], preferred_element_type=F32)
            for k in range(SPREAD):
                normed[pl.ds(pl.multiple_of(k * 128 + r * QUART, QUART), QUART), cols] = block[
                    k * QUART:(k + 1) * QUART].astype(BF16)
            col = col + jnp.sum(block * block, axis=1, keepdims=True)
        sq_own[r] = jnp.broadcast_to(jnp.sum(jnp.where(eye, col, 0.0), axis=0, keepdims=True), (8, 128))
        return c

    def sq_copy(d):
        return pltpu.make_async_remote_copy(
            src_ref=sq_own, dst_ref=sq_got.at[3 - d], send_sem=sqs.at[0], recv_sem=sqr.at[0],
            device_id=(dp, wrap(t + d, 4)), device_id_type=MESH)

    gain = jnp.concatenate([gain_ref[i:i + 1, :].astype(F32) for i in range(width // 128)], axis=1)

    def norm_rows(r, c):
        total = sq_own[r] + sq_got[0, r] + sq_got[1, r] + sq_got[2, r]
        scale = lax.rsqrt(total[0:1] / (width * TENSOR) + epsilon)
        col = jnp.sum(jnp.where(eye, scale, 0.0), axis=1, keepdims=True)
        for k in range(SPREAD):
            rows = pl.ds(pl.multiple_of(k * 128 + r * QUART, QUART), QUART)
            block = normed[rows, :].astype(F32) * col[k * QUART:(k + 1) * QUART] * gain
            normed[rows, :] = block.astype(BF16)
        return c

    scale_q = 1.0 / math.sqrt(HEAD)
    fresh_no = lax.broadcasted_iota(jnp.int32, (32, 8), 1)
    seen = jnp.logical_and(fresh_no % 2 == 0, fresh_no // 2 <= lax.broadcasted_iota(jnp.int32, (32, 8), 0) // 8)
    cache_no = lax.broadcasted_iota(jnp.int32, (1, 1024), 1)

    def order_queries(layer):
        for head in range(2):
            for step in range(4):
                for g in range(8):
                    begin = (head * 8 + g) * HEAD
                    q_rows[layer * 2 + head, pl.ds(step * 8 + g, 4, stride=32), :] = q_ref[
                        step, layer, :, begin:begin + HEAD].astype(F32)

    def attend_row(layer, head, r):
        q = q_rows[layer * 2 + head, r * 32:(r + 1) * 32, :]
        both = kv_ref[layer, r, :, :, head * HEAD:(head + 1) * HEAD].reshape(1024, HEAD)
        new = fresh_ref[:, layer, r, :, head * HEAD:(head + 1) * HEAD].astype(F32).reshape(8, HEAD)
        valid = jnp.logical_and(cache_no % 2 == 0, cache_no < 2 * meta_ref[0, r:r + 1, 0:1])
        cs = jnp.where(valid, dot_nt(q.astype(BF16), both) * scale_q, masked_score)
        fs = jnp.where(seen, dot_nt(q, new) * scale_q, masked_score)
        peak = jnp.maximum(jnp.max(cs, axis=1, keepdims=True), jnp.max(fs, axis=1, keepdims=True))
        ce = jnp.exp(cs - peak)
        fe = jnp.exp(fs - peak)
        total = jnp.sum(ce, axis=1, keepdims=True) + jnp.sum(fe, axis=1, keepdims=True)
        cw = pltpu.roll(ce / total, 1, 1).astype(BF16)
        fw = (fe / total).astype(BF16).astype(F32)
        res = jnp.dot(cw, both, preferred_element_type=F32)
        res = res + jnp.dot(fw, pltpu.roll(new, 7, 0), preferred_element_type=F32)
        for step in range(4):
            by_row[(step * 4 + r) * 8:(step * 4 + r + 1) * 8, :] = res[step * 8:(step + 1) * 8]

    def attend_end(layer, head):
        for g in range(8):
            begin = layer * width + head * 8 * HEAD + g * HEAD
            heads_ref[:, begin:begin + HEAD] = by_row[pl.ds(g, 16, stride=8), :].astype(BF16)

    def units(begin, end):
        for u in range(begin, end):
            attend_row(u // 8, (u // 4) % 2, u % 4)
            if u % 4 == 3:
                attend_end(u // 8, (u // 4) % 2)

    def direction(k):
        return 1 if k >= 2 else -1

    def project(part, owner, row0):
        zl = lax.div(owner, 2)
        ys = [lax.rem(owner, 2) * 2 + y_lo for y_lo in range(2)]
        wa = jnp.concatenate([gw[part][0, y, :, zl].reshape(128, half_w) for y in ys], axis=0)
        wb = jnp.concatenate([gw[part][1, :, y, zl].reshape(128, half_w) for y in ys], axis=0)
        rows = pl.ds(row0, 256)
        pacc[rows, :] = dot_nt(normed[rows, :half_w], wa) + dot_nt(normed[rows, half_w:], wb)

    def rs_copy(part, k, step):
        return pltpu.make_async_remote_copy(
            src_ref=rs_send.at[part, k, step], dst_ref=rs_recv.at[part, k, step], send_sem=rss.at[0],
            recv_sem=rsr.at[part, k, step], device_id=(dp, wrap(t + direction(k) * (1 if step else -1), 4)), device_id_type=MESH)

    def rot_copy(k):
        return pltpu.make_async_remote_copy(
            src_ref=whole.at[k - 1], dst_ref=scored_ref.at[pl.ds(k * 128, 128), :], send_sem=rot_s.at[0],
            recv_sem=rot_r.at[0], device_id=(lax.rem(dp + k, groups), t), device_id_type=MESH)

    def project_step(part, step):
        def both(i, c):
            project(part, wrap(t + (1 - 2 * i) * (1 + step), 4), pl.multiple_of(i * 256, 256))
            return c

        lax.fori_loop(0, 2, both, 0)

    def pass_step(part, step, ks):
        for k in ks:
            total = pacc[k * 128:(k + 1) * 128, :]
            for other in {2: (1,), 3: (0, 2)}.get(step, ()):
                got = rs_recv.at[part, k, other]
                pltpu.make_async_copy(got, got, rsr.at[part, k, other]).wait()
                total = total + got[...].astype(F32)
            total = total.astype(BF16)
            if step < 3:
                rs_send[part, k, step] = total
                rs_copy(part, k, step).start()
            elif part == 0:
                first_part[k] = total
            else:
                rows = jnp.dot(first_part[k], place_cols[0], preferred_element_type=F32)
                rows = (rows + jnp.dot(total, place_cols[1], preferred_element_type=F32)).astype(BF16)
                if k == 0:
                    scored_ref[0:128, :] = rows
                else:
                    whole[k - 1] = rows
                    rot_copy(k).start()

    line_no = lax.broadcasted_iota(jnp.int32, (256, 512), 0)
    goal_no = lax.broadcasted_iota(jnp.int32, (256, 512), 1)
    for part in range(2):
        goal = line_no // 16 * 32 + part * 16 + jnp.bitwise_and(line_no, 15)
        place_cols[part] = jnp.where(goal == goal_no, 1.0, 0.0).astype(BF16)

    def sums(part, step):
        project_step(part, step)
        pass_step(part, step, (3, 1, 2, 0))

    order_queries(0)
    order_queries(1)
    gath_a.after_z()
    resp_in.wait()
    lax.fori_loop(0, ROWS_G, turn_rows, 0)
    for d in (1, 2, 3):
        sq_copy(d).start()
    gath_a.after_first(1)
    gath_a.after_first(2)
    kv_in.wait()
    units(0, 2)
    gath_a.after_first(3)
    units(2, 3)
    gath_a.after_second(0)
    gath_a.after_second(1)
    units(3, 4)
    gath_b.after_z()
    gath_a.after_second(2)
    gath_a.after_second(3)
    wait_all(sq_got, sqs)
    wait_all(sq_got, sqr)
    lax.fori_loop(0, ROWS_G, norm_rows, 0)
    gath_b.after_first(1)
    gath_b.after_first(2)
    for i in range(4):
        gath_a.after_onward(i)
    gath_b.after_first(3)
    gath_a.after_across()
    sums(0, 1)
    sums(0, 0)
    gath_b.after_second(0)
    units(4, 7)
    gath_b.after_second(1)
    units(7, 10)
    gath_b.after_second(2)
    units(10, 13)
    gath_b.after_second(3)
    units(13, 16)
    gath_h.start()
    for i in range(4):
        gath_b.after_onward(i)
    gath_h.after_z()
    sums(0, 2)
    gath_b.after_across()
    sums(1, 1)
    gath_h.after_first(1)
    gath_h.after_first(2)
    sums(1, 0)
    gath_h.after_first(3)
    gath_h.after_second(0)
    sums(0, 3)
    gath_h.after_second(1)
    sums(1, 2)
    for i in (2, 3):
        gath_h.after_second(i)
    for i in (0, 1, 2, 3):
        gath_h.after_onward(i)
    gath_h.after_across()

    def decode_part(owner):
        zl = lax.div(owner, 2)
        ys = pl.ds(lax.rem(owner, 2) * 2, 2)
        a = jnp.dot(gh[0, ys, :, zl].reshape(256, width), outp_ref[0], preferred_element_type=F32)
        b = jnp.dot(gh[1, :, ys, zl].reshape(256, width), outp_ref[1], preferred_element_type=F32)
        b = jnp.concatenate([b[x * 64 + y * 32:x * 64 + y * 32 + 32] for y in range(2) for x in range(4)], axis=0)
        return a + b

    def ds_copy(d):
        return pltpu.make_async_remote_copy(
            src_ref=ds_send.at[d - 1], dst_ref=ds_recv.at[3 - d], send_sem=dss.at[0], recv_sem=dsr.at[0],
            device_id=(dp, wrap(t + d, 4)), device_id_type=MESH)

    outp_in.wait()
    for d in (2, 1, 3):
        ds_send[d - 1] = decode_part(wrap(t + d, 4)).astype(BF16)
        ds_copy(d).start()
    dacc[...] = decode_part(t)
    project_step(1, 3)
    pass_step(1, 3, (3, 1))
    wait_all(ds_recv, dsr)
    total = dacc[...]
    for d in range(3):
        total = total + ds_recv[d].astype(F32)
    dfin[...] = total.astype(BF16).reshape(16, 16, 128)

    mine = dec_ref.at[:, pl.ds(pl.multiple_of(dp * 128, 128), 128)]

    def message(i, dest_t):
        return pltpu.make_async_remote_copy(
            src_ref=dfin.at[i], dst_ref=mine, send_sem=out_s.at[0], recv_sem=out_r.at[0],
            device_id=(t * 16 + i, dest_t), device_id_type=MESH)

    for off in (2, 1, 3):
        for i in range(16):
            message(i, wrap(t + off, 4)).start()
    for i in range(16):

        @pl.when(t * 16 + i == dp)
        def _():
            pltpu.make_async_copy(dfin.at[i], mine, out_r.at[0]).start()

        @pl.when(t * 16 + i != dp)
        def _():
            message(i, t).start()

    pass_step(1, 3, (2, 0))
    wait_all(scored_ref.at[pl.ds(128, 384), :], rot_r)
    wait_all(whole, rot_s)
    wait_all(dec_ref, out_r)

    @pl.when(is_self)
    def _():
        wait_all(dec_ref.at[:, pl.ds(0, 63 * 128)], out_s)

    @pl.when(jnp.logical_not(is_self))
    def _():
        wait_all(dec_ref, out_s)

    wait_all(rs_send, rss)
    wait_all(ds_send, dss)
    gath_a.end()
    gath_b.end()
    gath_h.end()


def exchange(meta, q, fresh, gain, kv_cache, out_proj, resp_act, wt):
    width = wt.shape[1]
    vmem = pl.BlockSpec(memory_space=pltpu.VMEM)
    dma = pltpu.SemaphoreType.DMA
    return pl.pallas_call(
        kernel,
        out_shape=(
            jax.ShapeDtypeStruct((16, 8192), BF16),
            jax.ShapeDtypeStruct((512, 512), BF16),
        ),
        in_specs=[vmem] * 4 + [pl.BlockSpec(memory_space=pl.ANY)] * 4,
        out_specs=(vmem, vmem),
        scratch_shapes=[
            pltpu.VMEM(kv_cache.shape, BF16),
            pltpu.VMEM(out_proj.shape, BF16),
            pltpu.VMEM(resp_act.shape, BF16),
            pltpu.VMEM((4, 128, 128), F32),
            pltpu.VMEM((16, 2 * width), BF16),
            pltpu.VMEM((128, 128), F32),
            pltpu.VMEM((2, 4, 4, 2, 2, 16, width // 2), BF16),
            pltpu.VMEM((2, 4, 4, 2, 2, 16, width // 2), BF16),
            pltpu.VMEM((2, 4, 4, 2, 2, 16, width), BF16),
            pltpu.VMEM((512, width), BF16),
            pltpu.VMEM((512, 256), F32),
            pltpu.VMEM((2, 4, 3, 128, 256), BF16),
            pltpu.VMEM((2, 4, 3, 128, 256), BF16),
            pltpu.VMEM((4, 128, 256), BF16),
            pltpu.VMEM((3, 128, 512), BF16),
            pltpu.VMEM((2, 256, 512), BF16),
            pltpu.VMEM((256, 128), F32),
            pltpu.VMEM((3, 256, 128), BF16),
            pltpu.VMEM((3, 256, 128), BF16),
            pltpu.VMEM((16, 16, 128), BF16),
            pltpu.VMEM((4, 8, 128), F32),
            pltpu.VMEM((3, 4, 8, 128), F32),
            dma((6,)), dma((2, 17)), dma((1,)), dma((2,)),
            dma((6,)), dma((2, 17)), dma((1,)), dma((2,)),
            dma((6,)), dma((2, 17)), dma((1,)), dma((2,)),
            dma((1,)), dma((2, 4, 3)), dma((1,)), dma((1,)),
            dma((1,)), dma((1,)), dma((1,)), dma((1,)), dma((1,)), dma((1,)), dma((3,)),
        ],
        compiler_params=pltpu.CompilerParams(
            collective_id=0, has_side_effects=True, vmem_limit_bytes=56 * 1024 * 1024),
    )(meta, q, fresh, gain, kv_cache, out_proj, resp_act, wt)


def shards(
    queries,
    fresh_kv,
    kv_cache,
    cache_len,
    out_proj,
    finished,
    resp_len,
    start_shard,
    resp_act,
    reward_gain,
    reward_weight,
):
    steps, layers, rows, width = queries.shape
    meta = jnp.stack([cache_len, finished, resp_len, start_shard])
    meta = jnp.broadcast_to(meta[:, :, None], (4, rows, 128))
    dec, scored = exchange(
        meta, queries, fresh_kv, reward_gain.reshape(-1, 128), kv_cache, out_proj, resp_act, reward_weight.T
    )
    return dec.reshape(steps, rows, -1), scored


def solution(mesh):
    return jax.shard_map(
        shards,
        mesh=mesh,
        in_specs=(
            P(None, None, "dp", "tensor"),
            P(None, None, "dp", None, "tensor"),
            P(None, "dp", None, None, "tensor"),
            P("dp"),
            P(None, "tensor", "dp"),
            P("dp"),
            P("dp"),
            P("dp"),
            P("dp", None, "tensor"),
            P("tensor"),
            P("tensor", "dp"),
        ),
        out_specs=(P(None, "dp", None), P("dp", "tensor")),
        check_vma=False,
    )
```
